128 devices in a mesh: row: 8 (over z, core), col: 16 (over x, y).
Axes of the slice: x: 4, y: 4, z: 4, core: 2. Of those that a mesh axis runs over, the one named last changes fastest.
Arguments:
- embeddings: float32 [32768, 768], P(('row', 'col'))
- labels: int32 [32768], P(('row', 'col')), may hold values from 0 to 1, as said below
- source_id: int32 [32768], P(('row', 'col')), may hold values from 0 to 32767, as said below
Outputs:
- proof: float32 [32768], P(('row', 'col'))
- mmd_value: float32 [], replicated
The draws below stay inside these ranges and needn't reach their ends.
Inputs may be any that keep to these rules, and one draw needn't show every extreme that they name: `labels`: exactly 16384 samples carry 1. `source_id`: every sample id appears once; at a position of grid block b (positions b * 256 to (b + 1) * 256 - 1) the id's remainder modulo 256, divided by 2 and rounded down, equals b.
All inputs are finite; a program needn't handle non-finite values.
Results may differ from the reference program's by a relative error of at most 0.00007.
Values sent between devices are 32-bit elements; how exact they have to be, the bound alone decides.
A program may use at most 128 MiB of HBM per device.

```python
import math
import jax
import jax.numpy as jnp
from jax import lax

D = 768
PER_PEER = 2
BLOCKS = 128
SAMP_DEV = 256
SAMPLES = 32768


def label_table(key):
    order = jax.random.permutation(jax.random.fold_in(key, 11), SAMPLES)
    return (order >= SAMPLES // 2).astype(jnp.int32)


def draw_labels(key, part):
    return label_table(key)


def draw_embeddings(key, part):
    labels = label_table(key)
    clusters = SAMPLES // 128
    pick_a = jax.random.randint(jax.random.fold_in(key, 41), (SAMPLES,), 0, clusters)
    pick_b = jax.random.randint(jax.random.fold_in(key, 42), (SAMPLES,), 0, clusters)
    cluster_id = jnp.where(labels == 1, jnp.minimum(pick_a, pick_b), jnp.maximum(pick_a, pick_b))
    sub_id = cluster_id * 4 + jax.random.randint(jax.random.fold_in(key, 43), (SAMPLES,), 0, 4)
    first = jax.random.fold_in(key, 21)
    second = jax.random.fold_in(key, 22)
    third = jax.random.fold_in(key, 23)
    fourth = jax.random.fold_in(key, 24)
    centres = jax.random.normal(first, (clusters, D), jnp.float32)
    subs = jax.random.normal(second, (clusters * 4, D), jnp.float32)
    noise = jax.random.normal(third, (SAMPLES, D), jnp.float32)
    row_scale = jnp.exp(jax.random.uniform(fourth, (SAMPLES, 1), jnp.float32, math.log(0.7), math.log(1.4)))
    result = centres[cluster_id] * math.sqrt(600.0 / D) + subs[sub_id] * math.sqrt(150.0 / D)
    result = result + row_scale * noise * math.sqrt(50.0 / D)
    return result.astype(jnp.float32)


def draw_source_id(key, part):
    block_keys = jax.random.split(jax.random.fold_in(key, 31), BLOCKS)
    shuffles = jax.vmap(lambda one_key: jax.random.permutation(one_key, SAMP_DEV))(block_keys)
    owner_dev = shuffles // PER_PEER
    slot_idx = shuffles % PER_PEER
    block_idx = jnp.arange(BLOCKS, dtype=jnp.int32)[:, None]
    result = owner_dev * SAMP_DEV + block_idx * PER_PEER + slot_idx
    return result.reshape(-1).astype(jnp.int32)


def setup_inputs(seed: int = 0) -> dict:
    keys = jax.random.split(jax.random.key(seed), 4)
    embeddings = draw_embeddings(jax.random.fold_in(keys[3], 71), 0)
    labels = draw_labels(jax.random.fold_in(keys[3], 71), 0)
    source_id = draw_source_id(jax.random.fold_in(keys[3], 71), 0)
    return {"embeddings": embeddings, "labels": labels, "source_id": source_id}


def block_proof(query_rows, query_norm, key_rows, key_norm, key_sign):
    inner_prod = lax.dot_general(query_rows, key_rows, (((1,), (1,)), ((), ())), precision=lax.Precision.HIGHEST, preferred_element_type=jnp.float32)
    sq_dist = query_norm[:, None] + key_norm[None, :] - 2.0 * inner_prod
    kernel = jnp.exp(sq_dist * (-1.0 / 200.0))
    return jnp.dot(kernel, key_sign, precision=lax.Precision.HIGHEST, preferred_element_type=jnp.float32)


def reference(embeddings, labels, source_id):
    set_sign = (1 - 2 * labels).astype(jnp.float32)
    grid_emb = embeddings[source_id.astype(jnp.int32)]
    grid_sign = set_sign[source_id.astype(jnp.int32)]
    sq_norm = jnp.sum(grid_emb * grid_emb, axis=1)
    half_count = SAMPLES // 2
    query_blocks = grid_emb.reshape(-1, 512, D)
    norm_blocks = sq_norm.reshape(-1, 512)

    def one_block(pair):
        return block_proof(pair[0], pair[1], grid_emb, sq_norm, grid_sign)

    sums = lax.map(one_block, (query_blocks, norm_blocks)).reshape(-1)
    proof = sums * (1000.0 / half_count)
    mmd_value = jnp.sum(grid_sign * proof) * (1.0 / half_count)
    return proof, mmd_value
```

```python
import functools
import math

import jax
import jax.numpy as jnp
from jax import lax
from jax.experimental import pallas as pl
from jax.experimental.pallas import tpu as pltpu
from jax.sharding import PartitionSpec as P

MESH = pl.DeviceIdType.MESH
D = 768
ROWS = 256
AUX = 8
CHUNKS = 4
CORES = 2
ROWS_MESH = 8
COLS_MESH = 16
HALF_COUNT = 16384
SCALE = math.sqrt(2.0 * math.log2(math.e) / 200.0)

DIRS = [(1, 0, 0), (3, 0, 0), (0, 1, 0), (0, 3, 0), (0, 0, 1), (0, 0, 3)]
EDGES = [
    ((0, 0, 0), (3, 0, 0)), ((0, 0, 0), (1, 0, 0)), ((0, 0, 0), (0, 1, 0)),
    ((0, 0, 0), (0, 0, 1)), ((1, 0, 0), (2, 0, 0)), ((0, 1, 0), (0, 1, 3)),
    ((0, 0, 1), (0, 0, 2)), ((3, 0, 0), (3, 3, 0)), ((2, 0, 0), (2, 3, 0)),
    ((0, 1, 3), (0, 2, 3)), ((0, 2, 3), (0, 2, 2)),
]
ORDER = [
    (0, 0, 0), (3, 0, 0), (1, 0, 0), (0, 1, 0), (0, 0, 1), (0, 1, 3), (3, 3, 0),
    (0, 0, 2), (2, 0, 0), (0, 2, 3), (2, 3, 0), (0, 2, 2),
]
COUNT = len(ORDER)
SLOTS = CORES * COUNT
INDEX = {e: i for i, e in enumerate(ORDER)}
STEP = ROWS // CHUNKS


def minus(a, b):
    return tuple((u - v) % 4 for u, v in zip(a, b))


def pair_table():
    seen, table = set(), []
    for j in range(COUNT):
        full, half = [], []
        for i in range(j):
            diff = minus(ORDER[j], ORDER[i])
            kind = min(diff, minus((0, 0, 0), diff))
            if kind in seen:
                continue
            seen.add(kind)
            if all(v % 2 == 0 for v in kind):
                half.append((i, [t for t in range(3) if diff[t] == 2][0]))
            else:
                full.append(i)
        table.append((full, half))
    return table


CHILDREN = {i: [INDEX[w] for u, w in EDGES if INDEX[u] == i] for i in range(COUNT)}
PARENT = {INDEX[w]: INDEX[u] for u, w in EDGES}
PAIRS = pair_table()


def span(chunk):
    start = chunk * STEP
    return pl.ds(start, STEP + (AUX if chunk == CHUNKS - 1 else 0))


def product(a, b):
    dims = (((1,), (1,)), ((), ()))

    def dot(u, v):
        return lax.dot_general(u, v, dims, preferred_element_type=jnp.float32)

    return dot(a[:, :D], b[:, :D]) + dot(a[:, :D], b[:, D:]) + dot(a[:, D:], b[:, :D])


def kernel(
    emb, lab, src, out, mmd,
    raw, split, cols, row_acc, col_acc, part, part_in, every,
    load_sem, tree_send, tree_recv, sib_send, sib_recv, part_send, part_recv,
    col_send, col_recv, row_send, row_recv,
):
    row, col = lax.axis_index("row"), lax.axis_index("col")
    place = (col // 4, col % 4, row // 2)
    core = row % 2
    me = row * COLS_MESH + col

    def device(offset, flip=False):
        x, y, z = ((p + o) % 4 for p, o in zip(place, offset))
        c = (1 - core) if flip else core
        return (z * 2 + c, x * 4 + y)

    load = pltpu.make_async_copy(emb, raw.at[0, pl.ds(0, ROWS)], load_sem)
    load.start()
    barrier = pltpu.get_barrier_semaphore()
    for offset in DIRS:
        pl.semaphore_signal(barrier, inc=1, device_id=device(offset), device_id_type=MESH)
    pl.semaphore_signal(barrier, inc=1, device_id=device((0, 0, 0), True), device_id_type=MESH)

    load.wait()
    y = raw[0, pl.ds(0, ROWS)] * SCALE
    minus_half = -0.5 * jnp.sum(y * y, axis=1, keepdims=True)
    norm_row = jnp.transpose(jnp.broadcast_to(minus_half, (ROWS, 128)))[0:1]
    sign_row = (1 - 2 * lab[...]).astype(jnp.float32)
    aux = jnp.concatenate([norm_row, sign_row, jnp.zeros((AUX - 2, ROWS), jnp.float32)], axis=0)
    raw[0, pl.ds(ROWS, AUX)] = jnp.concatenate([aux, jnp.zeros((AUX, D - ROWS), jnp.float32)], axis=1)
    pl.semaphore_wait(barrier, 7)

    sent = []

    def relay(i, chunk):
        for w in CHILDREN[i]:
            back = minus(ORDER[i], ORDER[w])
            copy = pltpu.make_async_remote_copy(
                src_ref=raw.at[2 * i, span(chunk)],
                dst_ref=raw.at[2 * w, span(chunk)],
                send_sem=tree_send.at[w, chunk],
                recv_sem=tree_recv.at[w, chunk],
                device_id=device(back),
                device_id_type=MESH,
            )
            copy.start()
            sent.append(copy)

    def arrive(i, chunk):
        pltpu.make_async_remote_copy(
            src_ref=raw.at[2 * i, span(chunk)],
            dst_ref=raw.at[2 * i, span(chunk)],
            send_sem=tree_send.at[i, chunk],
            recv_sem=tree_recv.at[i, chunk],
            device_id=device(minus(ORDER[i], ORDER[PARENT[i]])),
            device_id_type=MESH,
        ).wait_recv()

    sibling = []

    def share(i):
        copy = pltpu.make_async_remote_copy(
            src_ref=raw.at[2 * i],
            dst_ref=raw.at[2 * i + 1],
            send_sem=sib_send.at[i],
            recv_sem=sib_recv.at[i],
            device_id=device((0, 0, 0), True),
            device_id_type=MESH,
        )
        copy.start()
        sent.append(copy)
        sibling.append(copy)

    def prepare(slot):
        @pl.loop(0, ROWS // 64)
        def _(t):
            rows = pl.ds(pl.multiple_of(t * 64, 64), 64)
            y = raw[slot, rows] * SCALE
            high = y.astype(jnp.bfloat16)
            split[slot, rows, :D] = high
            split[slot, rows, D:] = (y - high.astype(jnp.float32)).astype(jnp.bfloat16)
        if slot % 2 == 0:
            aux = raw[slot, pl.ds(ROWS, AUX), :ROWS]
            cols[slot // 2] = jnp.transpose(jnp.concatenate([aux] * (128 // AUX), axis=0))

    def work(i, slots, both):
        a = split[2 * i]
        norm_i, sign_i = cols[i, :, 0:1], cols[i, :, 1:2]
        for slot in slots:
            g = product(a, split[slot])
            aux = raw[slot, pl.ds(ROWS, AUX), :ROWS]
            e = jnp.exp2(g + norm_i + aux[0:1])
            q = e * aux[1:2]
            row_acc[i] += q[:, :128] + q[:, 128:]
            if both:
                col_acc[slot] += jnp.sum((e * sign_i).reshape(ROWS // 8, 8, ROWS), axis=0)

    for chunk in range(CHUNKS):
        relay(0, chunk)
    share(0)
    row_acc[...] = jnp.zeros_like(row_acc)
    col_acc[...] = jnp.zeros_like(col_acc)
    prepare(0)
    work(0, [0], False)
    sibling[0].wait_recv()
    prepare(1)
    work(0, [1], False)

    def take(i):
        for slot in (2 * i, 2 * i + 1):
            if slot % 2:
                sib_wait(i)
            prepare(slot)

    def sib_wait(i):
        pltpu.make_async_remote_copy(
            src_ref=raw.at[2 * i],
            dst_ref=raw.at[2 * i + 1],
            send_sem=sib_send.at[i],
            recv_sem=sib_recv.at[i],
            device_id=device((0, 0, 0), True),
            device_id_type=MESH,
        ).wait_recv()

    def pairs(i):
        full, half = PAIRS[i]
        if full:
            digits = sum(f << (4 * t) for t, f in enumerate(full))

            @pl.loop(0, len(full))
            def _(t):
                b = lax.shift_right_logical(jnp.int32(digits), jnp.int32(4 * t)) & 15
                work(i, [2 * b, 2 * b + 1], True)
        for b, axis in half:
            work(i, [2 * b + place[axis] // 2], True)

    def arrivals(level, chunk):
        for i in level:
            arrive(i, chunk)
            relay(i, chunk)

    levels = [[1, 2, 3, 4], [5, 6, 7, 8], [9, 10], [11]]
    for chunk in range(CHUNKS):
        arrivals(levels[0], chunk)
        if chunk >= 1:
            arrivals([5, 6], chunk - 1)
        if chunk >= 2:
            arrivals([9], chunk - 2)
    for i in levels[0]:
        share(i)
    for i in (1, 2):
        take(i)
        pairs(i)
    arrivals([5, 6], CHUNKS - 1)
    share(5)
    share(6)
    arrivals([8], 0)
    for i in (3, 4):
        take(i)
        pairs(i)
    arrivals([8], 1)
    arrivals([9], CHUNKS - 2)
    arrivals([9], CHUNKS - 1)
    for i in (5, 6):
        take(i)
        pairs(i)
    arrivals([8], 2)
    arrivals([8], 3)
    for i in (7, 9, 10, 11):
        if i in (9,):
            share(9)
            share(8)
            continue
        for chunk in range(CHUNKS):
            arrive(i, chunk)
        share(i)
    for i in (7, 8, 9, 10, 11):
        take(i)
        pairs(i)

    home = []
    for slot in range(SLOTS):
        i = slot // 2
        total = jnp.sum(col_acc[slot], axis=0, keepdims=True)
        if slot % 2 == 0:
            total = total + jnp.sum(jnp.transpose(row_acc[i]), axis=0, keepdims=True)
        part[slot] = total
        if slot:
            copy = pltpu.make_async_remote_copy(
                src_ref=part.at[slot],
                dst_ref=part_in.at[slot],
                send_sem=part_send.at[slot],
                recv_sem=part_recv.at[slot],
                device_id=device(ORDER[i], slot % 2 == 1),
                device_id_type=MESH,
            )
            copy.start()
            home.append(copy)
    proof = part[0]
    for t, copy in enumerate(home):
        copy.wait_recv()
        proof = proof + part_in[t + 1]
    proof = proof * (1000.0 / HALF_COUNT)
    here = jnp.sum(proof * sign_row, axis=1, keepdims=True)
    every[pl.ds(me, 1), :] = jnp.concatenate([proof, jnp.broadcast_to(here, (1, 128))], axis=1)

    copies = []
    for k in range(1, COLS_MESH):
        copy = pltpu.make_async_remote_copy(
            src_ref=every.at[pl.ds(me, 1)],
            dst_ref=every.at[pl.ds(me, 1)],
            send_sem=col_send.at[k],
            recv_sem=col_recv.at[k],
            device_id=(row, (col + k) % COLS_MESH),
            device_id_type=MESH,
        )
        copy.start()
        copies.append(copy)
    for k in range(1, COLS_MESH):
        other = row * COLS_MESH + (col + COLS_MESH - k) % COLS_MESH
        pltpu.make_async_remote_copy(
            src_ref=every.at[pl.ds(other, 1)],
            dst_ref=every.at[pl.ds(other, 1)],
            send_sem=col_send.at[k],
            recv_sem=col_recv.at[k],
            device_id=(row, (col + k) % COLS_MESH),
            device_id_type=MESH,
        ).wait_recv()
    for k in range(1, ROWS_MESH):
        block = pl.ds(pl.multiple_of(row * COLS_MESH, COLS_MESH), COLS_MESH)
        copy = pltpu.make_async_remote_copy(
            src_ref=every.at[block],
            dst_ref=every.at[block],
            send_sem=row_send.at[k],
            recv_sem=row_recv.at[k],
            device_id=((row + k) % ROWS_MESH, col),
            device_id_type=MESH,
        )
        copy.start()
        copies.append(copy)
    for k in range(1, ROWS_MESH):
        other = (row + ROWS_MESH - k) % ROWS_MESH
        block = pl.ds(pl.multiple_of(other * COLS_MESH, COLS_MESH), COLS_MESH)
        pltpu.make_async_remote_copy(
            src_ref=every.at[block],
            dst_ref=every.at[block],
            send_sem=row_send.at[k],
            recv_sem=row_recv.at[k],
            device_id=((row + k) % ROWS_MESH, col),
            device_id_type=MESH,
        ).wait_recv()

    proofs = every[:, :ROWS]
    lane = lax.broadcasted_iota(jnp.int32, proofs.shape, 1)
    first = jnp.sum(jnp.where(lane == 2 * me, proofs, 0.0), axis=1, keepdims=True)
    second = jnp.sum(jnp.where(lane == 2 * me + 1, proofs, 0.0), axis=1, keepdims=True)
    ids = src[...]
    owner = lax.broadcasted_iota(jnp.int32, proofs.shape, 0)
    value = jnp.where((ids & 1) == 0, first, second)
    out[...] = jnp.sum(jnp.where(owner == ids // ROWS, value, 0.0), axis=0, keepdims=True)
    total = jnp.sum(every[:, pl.ds(ROWS, 128)], axis=0, keepdims=True)
    mmd[...] = total * (1.0 / HALF_COUNT)
    for copy in sent + home + copies:
        copy.wait_send()


def local(embeddings, labels, source_id):
    vmem = pl.BlockSpec(memory_space=pltpu.VMEM)
    dma = pltpu.SemaphoreType.DMA
    f32 = jnp.float32
    proof, mmd = pl.pallas_call(
        kernel,
        out_shape=[
            jax.ShapeDtypeStruct((1, ROWS), f32),
            jax.ShapeDtypeStruct((1, 128), f32),
        ],
        in_specs=[pl.BlockSpec(memory_space=pl.ANY), vmem, vmem],
        out_specs=[vmem, vmem],
        scratch_shapes=[
            pltpu.VMEM((SLOTS, ROWS + AUX, D), f32),
            pltpu.VMEM((SLOTS, ROWS, 2 * D), jnp.bfloat16),
            pltpu.VMEM((COUNT, ROWS, 128), f32),
            pltpu.VMEM((COUNT, ROWS, 128), f32),
            pltpu.VMEM((SLOTS, 8, ROWS), f32),
            pltpu.VMEM((SLOTS, 1, ROWS), f32),
            pltpu.VMEM((SLOTS, 1, ROWS), f32),
            pltpu.VMEM((ROWS_MESH * COLS_MESH, ROWS + 128), f32),
            dma,
            dma((COUNT, CHUNKS)),
            dma((COUNT, CHUNKS)),
            dma((COUNT,)),
            dma((COUNT,)),
            dma((SLOTS,)),
            dma((SLOTS,)),
            dma((COLS_MESH,)),
            dma((COLS_MESH,)),
            dma((ROWS_MESH,)),
            dma((ROWS_MESH,)),
        ],
        compiler_params=pltpu.CompilerParams(
            collective_id=0, has_side_effects=True, vmem_limit_bytes=56 * 2**20
        ),
    )(embeddings, labels.reshape(1, ROWS), source_id.reshape(1, ROWS))
    return proof.reshape(ROWS), mmd[0, 0]


def solution(mesh):
    return jax.shard_map(
        local,
        mesh=mesh,
        in_specs=(P(("row", "col"), None), P(("row", "col")), P(("row", "col"))),
        out_specs=(P(("row", "col")), P()),
        check_vma=False,
    )
```

```python
import math

import jax
import jax.numpy as jnp
from jax import lax
from jax.experimental import pallas as pl
from jax.experimental.pallas import tpu as pltpu
from jax.sharding import PartitionSpec as P

MESH = pl.DeviceIdType.MESH
D = 768
ROWS = 256
AUX = 8
CORES = 2
ROWS_MESH = 8
COLS_MESH = 16
HALF_COUNT = 16384
SCALE = math.sqrt(2.0 * math.log2(math.e) / 200.0)

CHUNKS = 4
ORDER = [(0, 0, 0), (0, 0, 1), (0, 0, 3), (0, 3, 0), (3, 0, 0), (0, 1, 3), (1, 3, 0), (0, 0, 2), (0, 1, 2), (1, 2, 0), (2, 0, 0), (2, 2, 0)]
EDGES = [((0, 0, 0), (3, 0, 0)), ((0, 0, 0), (0, 0, 3)), ((0, 0, 0), (0, 3, 0)), ((0, 0, 0), (0, 0, 1)), ((0, 0, 3), (0, 1, 3)), ((0, 3, 0), (1, 3, 0)), ((3, 0, 0), (2, 0, 0)), ((0, 0, 1), (0, 0, 2)), ((0, 1, 3), (0, 1, 2)), ((1, 3, 0), (1, 2, 0)), ((1, 2, 0), (2, 2, 0))]
PLAN = [
    ('fwd', 1, 0),
    ('fwd', 2, 0),
    ('fwd', 3, 0),
    ('fwd', 4, 0),
    ('fwd', 1, 1),
    ('fwd', 2, 1),
    ('fwd', 3, 1),
    ('fwd', 4, 1),
    ('fwd', 5, 0),
    ('fwd', 6, 0),
    ('fwd', 1, 2),
    ('fwd', 2, 2),
    ('fwd', 3, 2),
    ('fwd', 4, 2),
    ('fwd', 5, 1),
    ('fwd', 6, 1),
    ('fwd', 1, 3),
    ('share', 1),
    ('fwd', 2, 3),
    ('share', 2),
    ('fwd', 3, 3),
    ('share', 3),
    ('fwd', 4, 3),
    ('share', 4),
    ('fwd', 5, 2),
    ('fwd', 6, 2),
    ('take', 1),
    ('full', 1, (0,)),
    ('take', 2),
    ('half', 2, (1,)),
    ('fwd', 9, 0),
    ('take', 3),
    ('full', 3, (0, 1)),
    ('fwd', 5, 3),
    ('share', 5),
    ('fwd', 6, 3),
    ('share', 6),
    ('full', 3, (2,)),
    ('take', 4),
    ('full', 4, (0, 1)),
    ('fwd', 9, 1),
    ('full', 4, (2, 3)),
    ('take', 5),
    ('full', 5, (1, 3)),
    ('fwd', 9, 2),
    ('full', 5, (4,)),
    ('take', 6),
    ('full', 6, (1, 2, 4, 5)),
    ('share', 7),
    ('share', 8),
    ('fwd', 9, 3),
    ('share', 9),
    ('share', 10),
    ('take', 7),
    ('full', 7, (4, 6)),
    ('take', 8),
    ('full', 8, (4, 6)),
    ('half', 8, (3,)),
    ('take', 9),
    ('full', 9, (0, 1)),
    ('share', 11),
    ('full', 9, (5,)),
    ('half', 9, (4,)),
    ('take', 10),
    ('full', 10, (1, 5, 6, 8)),
    ('half', 10, (0, 7)),
    ('take', 11),
    ('full', 11, (1, 5)),
    ('half', 11, (7, 10)),
]

DIRS = [(1, 0, 0), (3, 0, 0), (0, 1, 0), (0, 3, 0), (0, 0, 1), (0, 0, 3)]
COUNT = len(ORDER)
SLOTS = CORES * COUNT
INDEX = {e: i for i, e in enumerate(ORDER)}
STEP = ROWS // CHUNKS
CHILDREN = {i: [INDEX[w] for u, w in EDGES if INDEX[u] == i] for i in range(COUNT)}
PARENT = {INDEX[w]: INDEX[u] for u, w in EDGES}
FIRST_SEM = {}
SEMS = 0
for _i in range(1, COUNT):
    FIRST_SEM[_i] = SEMS
    SEMS += CHUNKS if CHILDREN[_i] else 1


def minus(a, b):
    return tuple((u - v) % 4 for u, v in zip(a, b))


def span(chunk):
    start = chunk * STEP
    return pl.ds(start, STEP + (AUX if chunk == CHUNKS - 1 else 0))


def product(a, b):
    dims = (((1,), (1,)), ((), ()))

    def dot(u, v):
        return lax.dot_general(u, v, dims, preferred_element_type=jnp.float32)

    return dot(a[:, :D], b[:, :D]) + dot(a[:, :D], b[:, D:]) + dot(a[:, D:], b[:, :D])


def kernel(
    emb, lab, src, out,
    raw, split, cols, row_acc, col_acc, part, part_in, stage, final,
    load_sem, tree_send, tree_recv, sib_send, sib_recv, part_send, part_recv,
    row_send, row_recv, col_send, col_recv,
):
    row, col = lax.axis_index("row"), lax.axis_index("col")
    place = (col // 4, col % 4, row // 2)
    core = row % 2
    me = row * COLS_MESH + col

    def device(offset, flip=False):
        x, y, z = ((p + o) % 4 if o else p for p, o in zip(place, offset))
        c = (1 - core) if flip else core
        return (z * 2 + c, x * 4 + y)

    other_core = device((0, 0, 0), True)

    def remote(source, target, send, recv, to):
        return pltpu.make_async_remote_copy(
            src_ref=source, dst_ref=target, send_sem=send, recv_sem=recv,
            device_id=to, device_id_type=MESH,
        )

    load = pltpu.make_async_copy(emb, raw.at[0, pl.ds(0, ROWS)], load_sem)
    load.start()
    barrier = pltpu.get_barrier_semaphore()
    for offset in DIRS:
        pl.semaphore_signal(barrier, inc=1, device_id=device(offset), device_id_type=MESH)
    pl.semaphore_signal(barrier, inc=1, device_id=other_core, device_id_type=MESH)

    load.wait()
    y = raw[0, pl.ds(0, ROWS)] * SCALE
    minus_half = -0.5 * jnp.sum(y * y, axis=1, keepdims=True)
    norm_row = jnp.transpose(jnp.broadcast_to(minus_half, (ROWS, 128)))[0:1]
    sign_row = (1 - 2 * lab[...]).astype(jnp.float32)
    aux = jnp.concatenate([norm_row, sign_row, jnp.zeros((AUX - 2, ROWS), jnp.float32)], axis=0)
    raw[0, pl.ds(ROWS, AUX)] = jnp.concatenate([aux, jnp.zeros((AUX, D - ROWS), jnp.float32)], axis=1)
    pl.semaphore_wait(barrier, 7)

    def relay(i, chunk):
        for w in CHILDREN[i]:
            sem = FIRST_SEM[w] + (chunk if CHILDREN[w] else 0)
            remote(
                raw.at[2 * i, span(chunk)], raw.at[2 * w, span(chunk)],
                tree_send, tree_recv.at[sem], device(minus(ORDER[i], ORDER[w])),
            ).start()

    def arrive(i, chunk):
        sem = FIRST_SEM[i] + (chunk if CHILDREN[i] else 0)
        rows = raw.at[2 * i, span(chunk)] if CHILDREN[i] else raw.at[2 * i]
        remote(rows, rows, tree_send, tree_recv.at[sem], other_core).wait_recv()

    def sibling(i):
        return remote(raw.at[2 * i], raw.at[2 * i + 1], sib_send, sib_recv.at[i], other_core)

    def prepare(slot):
        @pl.loop(0, ROWS // 64)
        def _(t):
            rows = pl.ds(pl.multiple_of(t * 64, 64), 64)
            y = raw[slot, rows] * SCALE
            high = y.astype(jnp.bfloat16)
            split[slot, rows, :D] = high
            split[slot, rows, D:] = (y - high.astype(jnp.float32)).astype(jnp.bfloat16)
        if slot % 2 == 0:
            aux = raw[slot, pl.ds(ROWS, AUX), :ROWS]
            cols[slot // 2] = jnp.transpose(jnp.concatenate([aux] * (128 // AUX), axis=0))

    def work(i, slots, both=True):
        a = split[2 * i]
        norm_i, sign_i = cols[i, :, 0:1], cols[i, :, 1:2]
        for slot in slots:
            g = product(a, split[slot])
            aux = raw[slot, pl.ds(ROWS, AUX), :ROWS]
            e = jnp.exp2(g + norm_i + aux[0:1])
            q = e * aux[1:2]
            row_acc[i] += q[:, :128] + q[:, 128:]
            if both:
                col_acc[slot] += jnp.sum((e * sign_i).reshape(ROWS // 8, 8, ROWS), axis=0)

    def full(i, partners):
        pairs = len(partners) // 2
        if pairs > 1:
            digits = sum(f << (4 * t) for t, f in enumerate(partners[:2 * pairs]))

            @pl.loop(0, pairs)
            def _(t):
                both = lax.shift_right_logical(jnp.int32(digits), jnp.int32(8 * t))
                b, c = both & 15, lax.shift_right_logical(both, jnp.int32(4)) & 15
                work(i, [2 * b, 2 * b + 1, 2 * c, 2 * c + 1])
        elif pairs:
            b, c = partners[:2]
            work(i, [2 * b, 2 * b + 1, 2 * c, 2 * c + 1])
        if len(partners) % 2:
            b = partners[-1]
            work(i, [2 * b, 2 * b + 1])

    def half(i, partners):
        slots = []
        for b in partners:
            diff = minus(ORDER[i], ORDER[b])
            axis = [t for t in range(3) if diff[t] == 2][0]
            slots.append(2 * b + place[axis] // 2)
        work(i, slots)

    for chunk in range(CHUNKS):
        relay(0, chunk)
    sibling(0).start()
    row_acc[...] = jnp.zeros_like(row_acc)
    col_acc[...] = jnp.zeros_like(col_acc)
    prepare(0)
    sibling(0).wait_recv()
    prepare(1)
    work(0, [0, 1], False)

    for op, i, *rest in PLAN:
        if op == "fwd":
            arrive(i, rest[0])
            relay(i, rest[0])
        elif op == "share":
            if not CHILDREN[i]:
                arrive(i, 0)
            sibling(i).start()
        elif op == "take":
            prepare(2 * i)
            sibling(i).wait_recv()
            prepare(2 * i + 1)
        elif op == "full":
            full(i, rest[0])
        else:
            half(i, rest[0])

    for slot in range(SLOTS):
        i = slot // 2
        total = jnp.sum(col_acc[slot], axis=0, keepdims=True)
        if slot % 2 == 0:
            total = total + jnp.sum(jnp.transpose(row_acc[i]), axis=0, keepdims=True)
        part[slot] = total
        if slot:
            remote(
                part.at[slot], part_in.at[slot], part_send, part_recv,
                device(ORDER[i], slot % 2 == 1),
            ).start()
    rest = pl.ds(1, SLOTS - 1)
    arrived = remote(part.at[rest], part_in.at[rest], part_send, part_recv, other_core)
    arrived.wait_recv()
    proof = part[0]
    for slot in range(1, SLOTS):
        proof = proof + part_in[slot]
    proof = proof * (1000.0 / HALF_COUNT)
    here = jnp.sum(proof * sign_row, axis=1, keepdims=True)
    stage[pl.ds(row, 1), :] = jnp.concatenate([proof, jnp.broadcast_to(here, (1, 128))], axis=1)

    for k in range(1, ROWS_MESH):
        mine = stage.at[pl.ds(row, 1)]
        remote(mine, mine, row_send, row_recv, ((row + k) % ROWS_MESH, col)).start()
    seven = remote(
        raw.at[0, pl.ds(0, ROWS_MESH - 1), pl.ds(0, ROWS + 128)],
        raw.at[0, pl.ds(0, ROWS_MESH - 1), pl.ds(0, ROWS + 128)],
        row_send, row_recv, other_core,
    )
    seven.wait_recv()
    window = jnp.where(row < ROWS_MESH // 2, stage[:, :128], stage[:, 128:256])
    column_total = jnp.sum(stage[:, 256:], axis=0, keepdims=True)
    lane = lax.broadcasted_iota(jnp.int32, (8, 128), 1)
    base = (row % 4) * 32
    window = jnp.where((lane >= base) & (lane < base + 32), window, column_total)
    block = final.at[pl.ds(pl.multiple_of(col * 8, 8), 8)]
    final[pl.ds(pl.multiple_of(col * 8, 8), 8), :] = window
    for k in range(1, COLS_MESH):
        remote(block, block, col_send, col_recv, (row, (col + k) % COLS_MESH)).start()
    fifteen = remote(
        raw.at[0, pl.ds(0, 120), pl.ds(0, 128)], raw.at[0, pl.ds(0, 120), pl.ds(0, 128)],
        col_send, col_recv, other_core,
    )
    fifteen.wait_recv()

    values = final[...]
    lane = lax.broadcasted_iota(jnp.int32, values.shape, 1)
    first = jnp.sum(jnp.where(lane == base + 2 * col, values, 0.0), axis=1, keepdims=True)
    second = jnp.sum(jnp.where(lane == base + 2 * col + 1, values, 0.0), axis=1, keepdims=True)
    ids = src[...]
    held = lax.broadcasted_iota(jnp.int32, (128, ROWS), 0)
    owner = (held % 8) * COLS_MESH + held // 8
    value = jnp.where((ids & 1) == 0, first, second)
    proofs = jnp.sum(jnp.where(owner == ids // ROWS, value, 0.0), axis=0, keepdims=True)
    unused = (base + 32) % 128
    sums = jnp.sum(jnp.where((lane == unused) & (held[:, :128] % 8 == 0), values, 0.0), axis=0, keepdims=True)
    total = jnp.sum(sums, axis=1, keepdims=True) * (1.0 / HALF_COUNT)
    out[...] = jnp.concatenate([proofs, jnp.broadcast_to(total, (1, 128))], axis=1)

    tree = raw.at[pl.ds(0, COUNT - 1)]
    remote(tree, tree, tree_send, load_sem, other_core).wait_send()
    shared = raw.at[pl.ds(0, COUNT)]
    remote(shared, shared, sib_send, load_sem, other_core).wait_send()
    arrived.wait_send()
    seven.wait_send()
    fifteen.wait_send()


def local(embeddings, labels, source_id):
    vmem = pl.BlockSpec(memory_space=pltpu.VMEM)
    dma = pltpu.SemaphoreType.DMA
    f32 = jnp.float32
    result = pl.pallas_call(
        kernel,
        out_shape=jax.ShapeDtypeStruct((1, ROWS + 128), f32),
        in_specs=[pl.BlockSpec(memory_space=pl.ANY), vmem, vmem],
        out_specs=vmem,
        scratch_shapes=[
            pltpu.VMEM((SLOTS, ROWS + AUX, D), f32),
            pltpu.VMEM((SLOTS, ROWS, 2 * D), jnp.bfloat16),
            pltpu.VMEM((COUNT, ROWS, 128), f32),
            pltpu.VMEM((COUNT, ROWS, 128), f32),
            pltpu.VMEM((SLOTS, 8, ROWS), f32),
            pltpu.VMEM((SLOTS, 1, ROWS), f32),
            pltpu.VMEM((SLOTS, 1, ROWS), f32),
            pltpu.VMEM((ROWS_MESH, ROWS + 128), f32),
            pltpu.VMEM((ROWS_MESH * COLS_MESH, 128), f32),
            dma, dma, dma((SEMS,)), dma, dma((COUNT,)), dma, dma, dma, dma, dma, dma,
        ],
        compiler_params=pltpu.CompilerParams(
            collective_id=0, has_side_effects=True, vmem_limit_bytes=56 * 2**20
        ),
    )(embeddings, labels.reshape(1, ROWS), source_id.reshape(1, ROWS))
    return result[0, :ROWS], result[0, ROWS]


def solution(mesh):
    return jax.shard_map(
        local,
        mesh=mesh,
        in_specs=(P(("row", "col"), None), P(("row", "col")), P(("row", "col"))),
        out_specs=(P(("row", "col")), P()),
        check_vma=False,
    )
```

```python
import math

import jax
import jax.numpy as jnp
from jax import lax
from jax.experimental import pallas as pl
from jax.experimental.pallas import tpu as pltpu
from jax.sharding import PartitionSpec as P

MESH = pl.DeviceIdType.MESH
D = 768
ROWS = 256
AUX = 8
CORES = 2
ROWS_MESH = 8
COLS_MESH = 16
HALF_COUNT = 16384
SCALE = math.sqrt(2.0 * math.log2(math.e) / 200.0)

CHUNKS = 4
ORDER = [(0, 0, 0), (0, 0, 1), (0, 0, 3), (0, 1, 0), (3, 0, 0), (1, 0, 3), (3, 3, 0), (0, 0, 2), (0, 2, 0), (1, 0, 2), (2, 3, 0), (2, 2, 0)]
EDGES = [((0, 0, 0), (0, 1, 0)), ((0, 0, 0), (0, 0, 3)), ((0, 0, 0), (3, 0, 0)), ((0, 0, 0), (0, 0, 1)), ((0, 0, 1), (0, 0, 2)), ((0, 1, 0), (0, 2, 0)), ((0, 0, 3), (1, 0, 3)), ((3, 0, 0), (3, 3, 0)), ((1, 0, 3), (1, 0, 2)), ((3, 3, 0), (2, 3, 0)), ((2, 3, 0), (2, 2, 0))]
PLAN = [
    ('fwd', 1, 0),
    ('fwd', 2, 0),
    ('fwd', 3, 0),
    ('fwd', 4, 0),
    ('fwd', 1, 1),
    ('fwd', 2, 1),
    ('fwd', 3, 1),
    ('fwd', 4, 1),
    ('fwd', 5, 0),
    ('fwd', 6, 0),
    ('fwd', 1, 2),
    ('fwd', 2, 2),
    ('fwd', 3, 2),
    ('fwd', 4, 2),
    ('fwd', 5, 1),
    ('fwd', 6, 1),
    ('fwd', 1, 3),
    ('share', 1),
    ('fwd', 2, 3),
    ('share', 2),
    ('fwd', 3, 3),
    ('share', 3),
    ('fwd', 4, 3),
    ('share', 4),
    ('go', 1, (), (), (1,)),
    ('fwd', 5, 2),
    ('go', 1, (0,), (), (2,)),
    ('fwd', 6, 2),
    ('go', 2, (), (1,), (3,)),
    ('fwd', 10, 0),
    ('go', 3, (0, 1, 2), (), (4,)),
    ('fwd', 5, 3),
    ('share', 5),
    ('go', 4, (0, 1, 2), (), ()),
    ('fwd', 6, 3),
    ('share', 6),
    ('fwd', 10, 1),
    ('go', 4, (3,), (), (5,)),
    ('go', 5, (1, 3, 4), (), ()),
    ('go', 6, (), (), (6,)),
    ('fwd', 10, 2),
    ('go', 6, (1, 2, 3, 5), (), ()),
    ('share', 7),
    ('share', 8),
    ('share', 9),
    ('fwd', 10, 3),
    ('share', 10),
    ('go', 7, (), (), (7,)),
    ('go', 7, (3, 6), (), (8,)),
    ('go', 8, (1, 5, 6), (0, 7), (9,)),
    ('go', 9, (3, 6, 8), (4,), (10,)),
    ('share', 11),
    ('go', 10, (0, 1, 5), (3,), ()),
    ('go', 11, (), (), (11,)),
    ('go', 11, (1, 5), (7, 8), ()),
]

DIRS = [(1, 0, 0), (3, 0, 0), (0, 1, 0), (0, 3, 0), (0, 0, 1), (0, 0, 3)]
COUNT = len(ORDER)
SLOTS = CORES * COUNT
INDEX = {e: i for i, e in enumerate(ORDER)}
STEP = ROWS // CHUNKS
CHILDREN = {i: [INDEX[w] for u, w in EDGES if INDEX[u] == i] for i in range(COUNT)}
FIRST_SEM = {}
SEMS = 0
for _i in range(1, COUNT):
    FIRST_SEM[_i] = SEMS
    SEMS += CHUNKS if CHILDREN[_i] else 1
STEPS = [p for p in PLAN if p[0] == "go"]
LAST = {i: max([0] + [k for k, p in enumerate(STEPS) if (p[1] == i and p[2] + p[3]) or i in p[2] + p[3]]) for i in range(COUNT)}


def minus(a, b):
    return tuple((u - v) % 4 for u, v in zip(a, b))


def span(chunk):
    start = chunk * STEP
    return pl.ds(start, STEP + (AUX if chunk == CHUNKS - 1 else 0))


def product(a, b):
    dims = (((1,), (1,)), ((), ()))

    def dot(u, v):
        return lax.dot_general(u, v, dims, preferred_element_type=jnp.float32)

    return dot(a[:, :D], b[:, :D]) + dot(a[:, :D], b[:, D:]) + dot(a[:, D:], b[:, :D])


def kernel(
    emb, lab_in, src_in, out,
    lab, src, raw, split, cols, row_acc, col_acc, part, part_in, stage, final,
    load_sem, lab_sem, src_sem, tree_send, tree_recv, sib_send, sib_recv, part_send, part_recv,
    row_send, row_recv, col_send, col_recv,
):
    row, col = lax.axis_index("row"), lax.axis_index("col")
    place = (col // 4, col % 4, row // 2)
    core = row % 2
    me = row * COLS_MESH + col

    def device(offset, flip=False):
        x, y, z = ((p + o) % 4 if o else p for p, o in zip(place, offset))
        c = (1 - core) if flip else core
        return (z * 2 + c, x * 4 + y)

    other_core = device((0, 0, 0), True)

    def remote(source, target, send, recv, to):
        return pltpu.make_async_remote_copy(
            src_ref=source, dst_ref=target, send_sem=send, recv_sem=recv,
            device_id=to, device_id_type=MESH,
        )

    load = pltpu.make_async_copy(emb, raw.at[0, pl.ds(0, ROWS)], load_sem)
    load.start()
    load_lab = pltpu.make_async_copy(lab_in, lab, lab_sem)
    load_lab.start()
    load_src = pltpu.make_async_copy(src_in, src, src_sem)
    load_src.start()
    barrier = pltpu.get_barrier_semaphore()
    for offset in DIRS:
        pl.semaphore_signal(barrier, inc=1, device_id=device(offset), device_id_type=MESH)
    pl.semaphore_signal(barrier, inc=1, device_id=other_core, device_id_type=MESH)

    load.wait()
    y = raw[0, pl.ds(0, ROWS)] * SCALE
    minus_half = -0.5 * jnp.sum(y * y, axis=1, keepdims=True)
    norm_row = jnp.transpose(jnp.broadcast_to(minus_half, (ROWS, 128)))[0:1]
    load_lab.wait()
    sign_row = (1 - 2 * lab[...]).astype(jnp.float32)
    aux = jnp.concatenate([norm_row, sign_row, jnp.zeros((AUX - 2, ROWS), jnp.float32)], axis=0)
    raw[0, pl.ds(ROWS, AUX)] = jnp.concatenate([aux, jnp.zeros((AUX, D - ROWS), jnp.float32)], axis=1)
    pl.semaphore_wait(barrier, 7)

    def relay(i, chunk):
        for w in CHILDREN[i]:
            sem = FIRST_SEM[w] + (chunk if CHILDREN[w] else 0)
            remote(
                raw.at[2 * i, span(chunk)], raw.at[2 * w, span(chunk)],
                tree_send, tree_recv.at[sem], device(minus(ORDER[i], ORDER[w])),
            ).start()

    def arrive(i, chunk):
        sem = FIRST_SEM[i] + (chunk if CHILDREN[i] else 0)
        rows = raw.at[2 * i, span(chunk)] if CHILDREN[i] else raw.at[2 * i]
        remote(rows, rows, tree_send, tree_recv.at[sem], other_core).wait_recv()

    def sibling(i):
        return remote(raw.at[2 * i], raw.at[2 * i + 1], sib_send, sib_recv.at[i], other_core)

    def prepare(slot):
        for start in range(0, ROWS, 32):
            rows = pl.ds(start, 32)
            y = raw[slot, rows] * SCALE
            high = y.astype(jnp.bfloat16)
            split[slot, rows, :D] = high
            split[slot, rows, D:] = (y - high.astype(jnp.float32)).astype(jnp.bfloat16)
        if slot % 2 == 0:
            aux = raw[slot, pl.ds(ROWS, AUX), :ROWS]
            cols[slot // 2] = jnp.transpose(jnp.concatenate([aux] * (128 // AUX), axis=0))

    def work(i, slots, both=True):
        a = split[2 * i]
        norm_i, sign_i = cols[i, :, 0:1], cols[i, :, 1:2]
        for slot in slots:
            g = product(a, split[slot])
            aux = raw[slot, pl.ds(ROWS, AUX), :ROWS]
            e = jnp.exp2(g + norm_i + aux[0:1])
            q = e * aux[1:2]
            row_acc[i] += q[:, :128] + q[:, 128:]
            if both:
                col_acc[slot] += jnp.sum((e * sign_i).reshape(ROWS // 8, 8, ROWS), axis=0)

    def half_slot(i, b):
        diff = minus(ORDER[i], ORDER[b])
        axis = [t for t in range(3) if diff[t] == 2][0]
        return 2 * b + place[axis] // 2

    def totals(i):
        for slot in (2 * i, 2 * i + 1):
            total = jnp.sum(col_acc[slot], axis=0, keepdims=True)
            if slot % 2 == 0:
                total = total + jnp.sum(jnp.transpose(row_acc[i]), axis=0, keepdims=True)
            part[slot] = total

    def send_totals(i):
        for slot in (2 * i, 2 * i + 1):
            if slot:
                remote(
                    part.at[slot], part_in.at[slot], part_send, part_recv,
                    device(ORDER[i], slot % 2 == 1),
                ).start()

    for chunk in range(CHUNKS):
        relay(0, chunk)
    sibling(0).start()
    row_acc[...] = jnp.zeros_like(row_acc)
    col_acc[...] = jnp.zeros_like(col_acc)
    prepare(0)
    sibling(0).wait_recv()
    prepare(1)
    work(0, [0, 1], False)

    step, sent = 0, set()
    for op in PLAN:
        if op[0] == "fwd":
            arrive(op[1], op[2])
            relay(op[1], op[2])
            continue
        if op[0] == "share":
            if not CHILDREN[op[1]]:
                arrive(op[1], 0)
            sibling(op[1]).start()
            continue
        _, i, full, half, fresh = op
        for w in fresh:
            sibling(w).wait_recv()
        done = [e for e in range(COUNT) if e not in sent and LAST[e] < step]
        for e in done:
            totals(e)
        for w in fresh:
            prepare(2 * w)
            prepare(2 * w + 1)
        work(i, [2 * b + t for b in full for t in range(CORES)] + [half_slot(i, b) for b in half])
        for e in done:
            send_totals(e)
        sent.update(done)
        step += 1
    for e in range(COUNT):
        if e not in sent:
            totals(e)
            send_totals(e)

    rest = pl.ds(1, SLOTS - 1)
    arrived = remote(part.at[rest], part_in.at[rest], part_send, part_recv, other_core)
    arrived.wait_recv()
    proof = part[0]
    for slot in range(1, SLOTS):
        proof = proof + part_in[slot]
    proof = proof * (1000.0 / HALF_COUNT)
    here = jnp.sum(proof * sign_row, axis=1, keepdims=True)
    stage[pl.ds(row, 1), :] = jnp.concatenate([proof, jnp.broadcast_to(here, (1, 128))], axis=1)

    for k in range(1, ROWS_MESH):
        mine = stage.at[pl.ds(row, 1)]
        remote(mine, mine, row_send, row_recv, ((row + k) % ROWS_MESH, col)).start()
    seven = remote(
        raw.at[0, pl.ds(0, ROWS_MESH - 1), pl.ds(0, ROWS + 128)],
        raw.at[0, pl.ds(0, ROWS_MESH - 1), pl.ds(0, ROWS + 128)],
        row_send, row_recv, other_core,
    )
    seven.wait_recv()
    window = jnp.where(row < ROWS_MESH // 2, stage[:, :128], stage[:, 128:256])
    column_total = jnp.sum(stage[:, 256:], axis=0, keepdims=True)
    lane = lax.broadcasted_iota(jnp.int32, (8, 128), 1)
    base = (row % 4) * 32
    window = jnp.where((lane >= base) & (lane < base + 32), window, column_total)
    block = final.at[pl.ds(pl.multiple_of(col * 8, 8), 8)]
    final[pl.ds(pl.multiple_of(col * 8, 8), 8), :] = window
    for k in range(1, COLS_MESH):
        remote(block, block, col_send, col_recv, (row, (col + k) % COLS_MESH)).start()
    fifteen = remote(
        raw.at[0, pl.ds(0, 120), pl.ds(0, 128)], raw.at[0, pl.ds(0, 120), pl.ds(0, 128)],
        col_send, col_recv, other_core,
    )
    fifteen.wait_recv()

    values = final[...]
    lane = lax.broadcasted_iota(jnp.int32, values.shape, 1)
    first = jnp.sum(jnp.where(lane == base + 2 * col, values, 0.0), axis=1, keepdims=True)
    second = jnp.sum(jnp.where(lane == base + 2 * col + 1, values, 0.0), axis=1, keepdims=True)
    load_src.wait()
    ids = src[...]
    held = lax.broadcasted_iota(jnp.int32, (128, ROWS), 0)
    owner = (held % 8) * COLS_MESH + held // 8
    value = jnp.where((ids & 1) == 0, first, second)
    proofs = jnp.sum(jnp.where(owner == ids // ROWS, value, 0.0), axis=0, keepdims=True)
    unused = (base + 32) % 128
    sums = jnp.sum(jnp.where((lane == unused) & (held[:, :128] % 8 == 0), values, 0.0), axis=0, keepdims=True)
    total = jnp.sum(sums, axis=1, keepdims=True) * (1.0 / HALF_COUNT)
    out[...] = jnp.concatenate([proofs, jnp.broadcast_to(total, (1, 128))], axis=1)

    tree = raw.at[pl.ds(0, COUNT - 1)]
    remote(tree, tree, tree_send, load_sem, other_core).wait_send()
    shared = raw.at[pl.ds(0, COUNT)]
    remote(shared, shared, sib_send, load_sem, other_core).wait_send()
    arrived.wait_send()
    seven.wait_send()
    fifteen.wait_send()


def local(embeddings, labels, source_id):
    vmem = pl.BlockSpec(memory_space=pltpu.VMEM)
    dma = pltpu.SemaphoreType.DMA
    f32 = jnp.float32
    result = pl.pallas_call(
        kernel,
        out_shape=jax.ShapeDtypeStruct((1, ROWS + 128), f32),
        in_specs=[pl.BlockSpec(memory_space=pl.ANY)] * 3,
        out_specs=vmem,
        scratch_shapes=[
            pltpu.VMEM((1, ROWS), jnp.int32),
            pltpu.VMEM((1, ROWS), jnp.int32),
            pltpu.VMEM((SLOTS, ROWS + AUX, D), f32),
            pltpu.VMEM((SLOTS, ROWS, 2 * D), jnp.bfloat16),
            pltpu.VMEM((COUNT, ROWS, 128), f32),
            pltpu.VMEM((COUNT, ROWS, 128), f32),
            pltpu.VMEM((SLOTS, 8, ROWS), f32),
            pltpu.VMEM((SLOTS, 1, ROWS), f32),
            pltpu.VMEM((SLOTS, 1, ROWS), f32),
            pltpu.VMEM((ROWS_MESH, ROWS + 128), f32),
            pltpu.VMEM((ROWS_MESH * COLS_MESH, 128), f32),
            dma, dma, dma, dma, dma((SEMS,)), dma, dma((COUNT,)), dma, dma, dma, dma, dma, dma,
        ],
        compiler_params=pltpu.CompilerParams(
            collective_id=0, has_side_effects=True, vmem_limit_bytes=56 * 2**20
        ),
    )(embeddings, labels.reshape(1, ROWS), source_id.reshape(1, ROWS))
    return result[0, :ROWS], result[0, ROWS]


def solution(mesh):
    return jax.shard_map(
        local,
        mesh=mesh,
        in_specs=(P(("row", "col"), None), P(("row", "col")), P(("row", "col"))),
        out_specs=(P(("row", "col")), P()),
        check_vma=False,
    )
```

```python
import math

import jax
import jax.numpy as jnp
from jax import lax
from jax.experimental import pallas as pl
from jax.experimental.pallas import tpu as pltpu
from jax.sharding import PartitionSpec as P

MESH = pl.DeviceIdType.MESH
D = 768
ROWS = 256
AUX = 8
CORES = 2
ROWS_MESH = 8
COLS_MESH = 16
HALF_COUNT = 16384
SCALE = math.sqrt(2.0 * math.log2(math.e) / 200.0)

SIZES = (32, 48, 56, 56, 64)
ORDER = [(0, 0, 0), (0, 0, 1), (0, 0, 3), (0, 1, 0), (3, 0, 0), (1, 0, 3), (3, 3, 0), (0, 0, 2), (0, 2, 0), (1, 0, 2), (2, 3, 0), (2, 2, 0)]
EDGES = [((0, 0, 0), (0, 1, 0)), ((0, 0, 0), (0, 0, 3)), ((0, 0, 0), (3, 0, 0)), ((0, 0, 0), (0, 0, 1)), ((0, 0, 1), (0, 0, 2)), ((0, 1, 0), (0, 2, 0)), ((0, 0, 3), (1, 0, 3)), ((3, 0, 0), (3, 3, 0)), ((1, 0, 3), (1, 0, 2)), ((3, 3, 0), (2, 3, 0)), ((2, 3, 0), (2, 2, 0))]
PLAN = [
    ('fwd', 1, 0),
    ('fwd', 2, 0),
    ('fwd', 3, 0),
    ('fwd', 4, 0),
    ('fwd', 1, 1),
    ('fwd', 2, 1),
    ('fwd', 3, 1),
    ('fwd', 4, 1),
    ('fwd', 5, 0),
    ('fwd', 6, 0),
    ('fwd', 1, 2),
    ('fwd', 2, 2),
    ('fwd', 3, 2),
    ('fwd', 4, 2),
    ('fwd', 5, 1),
    ('fwd', 6, 1),
    ('fwd', 1, 3),
    ('fwd', 2, 3),
    ('fwd', 3, 3),
    ('fwd', 4, 3),
    ('fwd', 5, 2),
    ('fwd', 6, 2),
    ('fwd', 1, 4),
    ('share', 1),
    ('fwd', 2, 4),
    ('share', 2),
    ('fwd', 3, 4),
    ('share', 3),
    ('fwd', 4, 4),
    ('share', 4),
    ('go', 1, (), (), (1,), ()),
    ('go', 1, (0,), (), (2,), ()),
    ('fwd', 5, 3),
    ('fwd', 10, 0),
    ('fwd', 6, 3),
    ('go', 3, (), (), (3,), (1,)),
    ('go', 2, (), (1,), (4,), (2,)),
    ('go', 3, (0, 1, 2), (), (), (3,)),
    ('fwd', 10, 1),
    ('go', 4, (0, 1, 2), (), (), (4,)),
    ('fwd', 5, 4),
    ('share', 5),
    ('fwd', 6, 4),
    ('share', 6),
    ('go', 4, (3,), (), (5,), ()),
    ('fwd', 10, 2),
    ('go', 5, (1, 3, 4), (), (6,), ()),
    ('go', 6, (1, 2, 3), (), (), (5,)),
    ('fwd', 10, 3),
    ('go', 6, (5,), (), (), (6,)),
    ('share', 7),
    ('share', 8),
    ('share', 9),
    ('fwd', 10, 4),
    ('share', 10),
    ('go', 7, (), (), (7,), ()),
    ('go', 7, (3, 6), (), (8,), ()),
    ('go', 8, (1, 5, 6), (0,), (9,), (7,)),
    ('go', 8, (), (7,), (10,), (8,)),
    ('go', 9, (3, 6, 8), (4,), (), ()),
    ('share', 11),
    ('go', 10, (0, 1, 5), (3,), (11,), ()),
    ('go', 11, (1, 5), (7, 8), (), ()),
]

DIRS = [(1, 0, 0), (3, 0, 0), (0, 1, 0), (0, 3, 0), (0, 0, 1), (0, 0, 3)]
COUNT = len(ORDER)
SLOTS = CORES * COUNT
INDEX = {e: i for i, e in enumerate(ORDER)}
CHUNKS = len(SIZES)
CHILDREN = {i: [INDEX[w] for u, w in EDGES if INDEX[u] == i] for i in range(COUNT)}
FIRST_SEM = {}
SEMS = 0
for _i in range(1, COUNT):
    FIRST_SEM[_i] = SEMS
    SEMS += CHUNKS if CHILDREN[_i] else 1
STEPS = [p for p in PLAN if p[0] == "go"]
SHARED = {0} | {b for p in STEPS for b in p[2] + p[3]}
LAST = {i: max([0] + [k for k, p in enumerate(STEPS) if (p[1] == i and p[2] + p[3]) or i in p[2] + p[3]]) for i in range(COUNT)}


def minus(a, b):
    return tuple((u - v) % 4 for u, v in zip(a, b))


def span(chunk):
    return pl.ds(sum(SIZES[:chunk]), SIZES[chunk] + (AUX if chunk == CHUNKS - 1 else 0))


def product(a, b):
    dims = (((1,), (1,)), ((), ()))

    def dot(u, v):
        return lax.dot_general(u, v, dims, preferred_element_type=jnp.float32)

    return dot(a[:, :D], b[:, :D]) + dot(a[:, :D], b[:, D:]) + dot(a[:, D:], b[:, :D])


def kernel(
    emb, lab_in, src_in, out,
    lab, src, raw, split, cols, row_acc, col_acc, part, part_in, stage, final,
    load_sem, lab_sem, src_sem, tree_send, tree_recv, sib_send, sib_recv, part_send, part_recv,
    row_send, row_recv, col_send, col_recv,
):
    row, col = lax.axis_index("row"), lax.axis_index("col")
    place = (col // 4, col % 4, row // 2)
    core = row % 2
    me = row * COLS_MESH + col

    def device(offset, flip=False):
        x, y, z = ((p + o) % 4 if o else p for p, o in zip(place, offset))
        c = (1 - core) if flip else core
        return (z * 2 + c, x * 4 + y)

    other_core = device((0, 0, 0), True)

    def remote(source, target, send, recv, to):
        return pltpu.make_async_remote_copy(
            src_ref=source, dst_ref=target, send_sem=send, recv_sem=recv,
            device_id=to, device_id_type=MESH,
        )

    load = pltpu.make_async_copy(emb, raw.at[0, pl.ds(0, ROWS)], load_sem)
    load.start()
    load_lab = pltpu.make_async_copy(lab_in, lab, lab_sem)
    load_lab.start()
    load_src = pltpu.make_async_copy(src_in, src, src_sem)
    load_src.start()
    barrier = pltpu.get_barrier_semaphore()
    for offset in DIRS:
        pl.semaphore_signal(barrier, inc=1, device_id=device(offset), device_id_type=MESH)
    pl.semaphore_signal(barrier, inc=1, device_id=other_core, device_id_type=MESH)

    load.wait()
    y = raw[0, pl.ds(0, ROWS)] * SCALE
    minus_half = -0.5 * jnp.sum(y * y, axis=1, keepdims=True)
    norm_row = jnp.transpose(jnp.broadcast_to(minus_half, (ROWS, 128)))[0:1]
    load_lab.wait()
    sign_row = (1 - 2 * lab[...]).astype(jnp.float32)
    aux = jnp.concatenate([norm_row, sign_row, jnp.zeros((AUX - 2, ROWS), jnp.float32)], axis=0)
    raw[0, pl.ds(ROWS, AUX)] = jnp.concatenate([aux, jnp.zeros((AUX, D - ROWS), jnp.float32)], axis=1)
    pl.semaphore_wait(barrier, 7)

    def relay(i, chunk):
        for w in CHILDREN[i]:
            sem = FIRST_SEM[w] + (chunk if CHILDREN[w] else 0)
            remote(
                raw.at[2 * i, span(chunk)], raw.at[2 * w, span(chunk)],
                tree_send, tree_recv.at[sem], device(minus(ORDER[i], ORDER[w])),
            ).start()

    def arrive(i, chunk):
        sem = FIRST_SEM[i] + (chunk if CHILDREN[i] else 0)
        rows = raw.at[2 * i, span(chunk)] if CHILDREN[i] else raw.at[2 * i]
        remote(rows, rows, tree_send, tree_recv.at[sem], other_core).wait_recv()

    def sibling(i):
        return remote(raw.at[2 * i], raw.at[2 * i + 1], sib_send, sib_recv.at[i], other_core)

    def prepare(slot):
        for start in range(0, ROWS, 32):
            rows = pl.ds(start, 32)
            y = raw[slot, rows] * SCALE
            high = y.astype(jnp.bfloat16)
            split[slot, rows, :D] = high
            split[slot, rows, D:] = (y - high.astype(jnp.float32)).astype(jnp.bfloat16)
        if slot % 2 == 0:
            aux = raw[slot, pl.ds(ROWS, AUX), :ROWS]
            cols[slot // 2] = jnp.transpose(jnp.concatenate([aux] * (128 // AUX), axis=0))

    def work(i, slots, both=True):
        a = split[2 * i]
        norm_i, sign_i = cols[i, :, 0:1], cols[i, :, 1:2]
        for slot in slots:
            g = product(a, split[slot])
            aux = raw[slot, pl.ds(ROWS, AUX), :ROWS]
            e = jnp.exp2(g + norm_i + aux[0:1])
            q = e * aux[1:2]
            row_acc[i] += q[:, :128] + q[:, 128:]
            if both:
                col_acc[slot] += jnp.sum((e * sign_i).reshape(ROWS // 8, 8, ROWS), axis=0)

    def half_slot(i, b):
        diff = minus(ORDER[i], ORDER[b])
        axis = [t for t in range(3) if diff[t] == 2][0]
        return 2 * b + place[axis] // 2

    def totals(i):
        for slot in (2 * i, 2 * i + 1):
            total = jnp.sum(col_acc[slot], axis=0, keepdims=True)
            if slot % 2 == 0:
                total = total + jnp.sum(jnp.transpose(row_acc[i]), axis=0, keepdims=True)
            part[slot] = total

    def send_totals(i):
        if i:
            rows = pl.ds(2 * i, 2)
            remote(
                part.at[rows], part_in.at[rows], part_send, part_recv, device(ORDER[i])
            ).start()

    for chunk in range(CHUNKS):
        relay(0, chunk)
    sibling(0).start()
    row_acc[...] = jnp.zeros_like(row_acc)
    col_acc[...] = jnp.zeros_like(col_acc)
    prepare(0)
    sibling(0).wait_recv()
    prepare(1)
    work(0, [0, 1], False)

    step, sent = 0, set()
    for op in PLAN:
        if op[0] == "fwd":
            arrive(op[1], op[2])
            relay(op[1], op[2])
            continue
        if op[0] == "share":
            if not CHILDREN[op[1]]:
                arrive(op[1], 0)
            if op[1] in SHARED:
                sibling(op[1]).start()
            continue
        _, i, full, half, own, other = op
        for w in other:
            sibling(w).wait_recv()
        done = [e for e in range(COUNT) if e not in sent and LAST[e] < step]
        for e in done:
            totals(e)
        for w in own:
            prepare(2 * w)
        for w in other:
            prepare(2 * w + 1)
        work(i, [2 * b + t for b in full for t in range(CORES)] + [half_slot(i, b) for b in half])
        for e in done:
            send_totals(e)
        sent.update(done)
        step += 1
    for e in range(COUNT):
        if e not in sent:
            totals(e)
            send_totals(e)

    rest = pl.ds(2, SLOTS - 2)
    arrived = remote(part.at[rest], part_in.at[rest], part_send, part_recv, other_core)
    arrived.wait_recv()
    mine, his = part[0], part[1]
    for i in range(1, COUNT):
        mine, his = mine + part_in[2 * i], his + part_in[2 * i + 1]
    mine, his = mine * (1000.0 / HALF_COUNT), his * (1000.0 / HALF_COUNT)
    his_sign = raw[1, pl.ds(ROWS, AUX), :ROWS][1:2]
    here = jnp.sum(mine * sign_row + his * his_sign, axis=1, keepdims=True)
    zero, one = jnp.where(core == 0, mine, his), jnp.where(core == 0, his, mine)
    tail = jnp.broadcast_to(here, (1, 128))
    stage[row] = jnp.concatenate(
        [jnp.concatenate([zero, tail], axis=1), jnp.concatenate([one, tail], axis=1)], axis=0
    )

    for k in range(1, ROWS_MESH):
        block = stage.at[row]
        remote(block, block, row_send, row_recv, ((row + k) % ROWS_MESH, col)).start()
    others = stage.at[pl.ds(1, ROWS_MESH - 1)]
    seven = remote(others, others, row_send, row_recv, other_core)
    seven.wait_recv()
    halves = [stage[2 * z] + stage[2 * z + 1] for z in range(ROWS_MESH // 2)]
    sums = jnp.concatenate(halves, axis=0)
    window = jnp.where(row < ROWS_MESH // 2, sums[:, :128], sums[:, 128:256])
    column_total = 0.5 * jnp.sum(sums[:, 256:], axis=0, keepdims=True)
    lane = lax.broadcasted_iota(jnp.int32, (8, 128), 1)
    base = (row % 4) * 32
    window = jnp.where((lane >= base) & (lane < base + 32), window, column_total)
    block = final.at[pl.ds(pl.multiple_of(col * 8, 8), 8)]
    final[pl.ds(pl.multiple_of(col * 8, 8), 8), :] = window
    for k in range(1, COLS_MESH):
        remote(block, block, col_send, col_recv, (row, (col + k) % COLS_MESH)).start()
    fifteen = remote(
        raw.at[0, pl.ds(0, 120), pl.ds(0, 128)], raw.at[0, pl.ds(0, 120), pl.ds(0, 128)],
        col_send, col_recv, other_core,
    )
    fifteen.wait_recv()

    values = final[...]
    lane = lax.broadcasted_iota(jnp.int32, values.shape, 1)
    first = jnp.sum(jnp.where(lane == base + 2 * col, values, 0.0), axis=1, keepdims=True)
    second = jnp.sum(jnp.where(lane == base + 2 * col + 1, values, 0.0), axis=1, keepdims=True)
    load_src.wait()
    ids = src[...]
    held = lax.broadcasted_iota(jnp.int32, (128, ROWS), 0)
    owner = (held % 8) * COLS_MESH + held // 8
    value = jnp.where((ids & 1) == 0, first, second)
    proofs = jnp.sum(jnp.where(owner == ids // ROWS, value, 0.0), axis=0, keepdims=True)
    unused = (base + 32) % 128
    sums = jnp.sum(jnp.where((lane == unused) & (held[:, :128] % 8 == 0), values, 0.0), axis=0, keepdims=True)
    total = jnp.sum(sums, axis=1, keepdims=True) * (1.0 / HALF_COUNT)
    out[...] = jnp.concatenate([proofs, jnp.broadcast_to(total, (1, 128))], axis=1)

    tree = raw.at[pl.ds(0, COUNT - 1)]
    remote(tree, tree, tree_send, load_sem, other_core).wait_send()
    shared = raw.at[pl.ds(0, len(SHARED))]
    remote(shared, shared, sib_send, load_sem, other_core).wait_send()
    arrived.wait_send()
    seven.wait_send()
    fifteen.wait_send()


def local(embeddings, labels, source_id):
    vmem = pl.BlockSpec(memory_space=pltpu.VMEM)
    dma = pltpu.SemaphoreType.DMA
    f32 = jnp.float32
    result = pl.pallas_call(
        kernel,
        out_shape=jax.ShapeDtypeStruct((1, ROWS + 128), f32),
        in_specs=[pl.BlockSpec(memory_space=pl.ANY)] * 3,
        out_specs=vmem,
        scratch_shapes=[
            pltpu.VMEM((1, ROWS), jnp.int32),
            pltpu.VMEM((1, ROWS), jnp.int32),
            pltpu.VMEM((SLOTS, ROWS + AUX, D), f32),
            pltpu.VMEM((SLOTS, ROWS, 2 * D), jnp.bfloat16),
            pltpu.VMEM((COUNT, ROWS, 128), f32),
            pltpu.VMEM((COUNT, ROWS, 128), f32),
            pltpu.VMEM((SLOTS, 8, ROWS), f32),
            pltpu.VMEM((SLOTS, 1, ROWS), f32),
            pltpu.VMEM((SLOTS, 1, ROWS), f32),
            pltpu.VMEM((ROWS_MESH, 2, ROWS + 128), f32),
            pltpu.VMEM((ROWS_MESH * COLS_MESH, 128), f32),
            dma, dma, dma, dma, dma((SEMS,)), dma, dma((COUNT,)), dma, dma, dma, dma, dma, dma,
        ],
        compiler_params=pltpu.CompilerParams(
            collective_id=0, has_side_effects=True, vmem_limit_bytes=56 * 2**20
        ),
    )(embeddings, labels.reshape(1, ROWS), source_id.reshape(1, ROWS))
    return result[0, :ROWS], result[0, ROWS]


def solution(mesh):
    return jax.shard_map(
        local,
        mesh=mesh,
        in_specs=(P(("row", "col"), None), P(("row", "col")), P(("row", "col"))),
        out_specs=(P(("row", "col")), P()),
        check_vma=False,
    )
```

```python
import math

import jax
import jax.numpy as jnp
from jax import lax
from jax.experimental import pallas as pl
from jax.experimental.pallas import tpu as pltpu
from jax.sharding import PartitionSpec as P

MESH = pl.DeviceIdType.MESH
D = 768
ROWS = 256
AUX = 8
CORES = 2
ROWS_MESH = 8
COLS_MESH = 16
HALF_COUNT = 16384
SCALE = math.sqrt(2.0 * math.log2(math.e) / 200.0)

SIZES = (32, 48, 56, 56, 64)
ORDER = [(0, 0, 0), (0, 0, 1), (0, 0, 3), (0, 3, 0), (3, 0, 0), (0, 1, 3), (1, 3, 0), (0, 0, 2), (0, 1, 2), (1, 2, 0), (2, 0, 0), (2, 2, 0)]
EDGES = [((0, 0, 0), (3, 0, 0)), ((0, 0, 0), (0, 0, 3)), ((0, 0, 0), (0, 3, 0)), ((0, 0, 0), (0, 0, 1)), ((0, 0, 3), (0, 1, 3)), ((0, 3, 0), (1, 3, 0)), ((3, 0, 0), (2, 0, 0)), ((0, 0, 1), (0, 0, 2)), ((0, 1, 3), (0, 1, 2)), ((1, 3, 0), (1, 2, 0)), ((1, 2, 0), (2, 2, 0))]
PLAN = [
    ('fwd', 1, 0),
    ('fwd', 2, 0),
    ('fwd', 3, 0),
    ('fwd', 4, 0),
    ('fwd', 1, 1),
    ('fwd', 2, 1),
    ('fwd', 3, 1),
    ('fwd', 4, 1),
    ('fwd', 5, 0),
    ('fwd', 6, 0),
    ('fwd', 1, 2),
    ('fwd', 2, 2),
    ('fwd', 3, 2),
    ('fwd', 4, 2),
    ('fwd', 5, 1),
    ('fwd', 6, 1),
    ('fwd', 1, 3),
    ('fwd', 2, 3),
    ('fwd', 3, 3),
    ('fwd', 4, 3),
    ('fwd', 5, 2),
    ('fwd', 6, 2),
    ('fwd', 1, 4),
    ('share', 1),
    ('fwd', 2, 4),
    ('share', 2),
    ('fwd', 3, 4),
    ('share', 3),
    ('fwd', 4, 4),
    ('share', 4),
    ('go', 1, (), (), (1,), ()),
    ('go', 1, (0,), (), (2,), ()),
    ('fwd', 5, 3),
    ('fwd', 6, 3),
    ('fwd', 9, 0),
    ('go', 3, (), (), (3,), (1,)),
    ('go', 2, (), (1,), (4,), (2,)),
    ('go', 3, (0, 1, 2), (), (), (3,)),
    ('fwd', 9, 1),
    ('go', 4, (0, 1, 2), (), (), (4,)),
    ('fwd', 5, 4),
    ('share', 5),
    ('fwd', 6, 4),
    ('share', 6),
    ('go', 4, (3,), (), (5,), ()),
    ('fwd', 9, 2),
    ('go', 5, (1, 3, 4), (), (6,), ()),
    ('go', 6, (1, 2, 4), (), (), (5,)),
    ('fwd', 9, 3),
    ('go', 6, (5,), (), (), (6,)),
    ('share', 7),
    ('share', 8),
    ('fwd', 9, 4),
    ('share', 9),
    ('share', 10),
    ('go', 7, (), (), (7,), ()),
    ('go', 7, (4, 6), (), (8,), ()),
    ('go', 8, (4, 6), (3,), (9,), (7,)),
    ('go', 9, (0, 1, 5), (4,), (10,), (8,)),
    ('go', 10, (1, 5, 6, 8), (0, 7), (), (10,)),
    ('share', 11),
    ('go', 11, (), (), (11,), ()),
    ('go', 11, (1, 5), (7, 10), (), ()),
]

DIRS = [(1, 0, 0), (3, 0, 0), (0, 1, 0), (0, 3, 0), (0, 0, 1), (0, 0, 3)]
COUNT = len(ORDER)
SLOTS = CORES * COUNT
INDEX = {e: i for i, e in enumerate(ORDER)}
CHUNKS = len(SIZES)
CHILDREN = {i: [INDEX[w] for u, w in EDGES if INDEX[u] == i] for i in range(COUNT)}
FIRST_SEM = {}
SEMS = 0
for _i in range(1, COUNT):
    FIRST_SEM[_i] = SEMS
    SEMS += CHUNKS if CHILDREN[_i] else 1
STEPS = [p for p in PLAN if p[0] == "go"]
SHARED = {0} | {b for p in STEPS for b in p[2] + p[3]}
LAST = {i: max([0] + [k for k, p in enumerate(STEPS) if (p[1] == i and p[2] + p[3]) or i in p[2] + p[3]]) for i in range(COUNT)}


def minus(a, b):
    return tuple((u - v) % 4 for u, v in zip(a, b))


def span(chunk):
    return pl.ds(sum(SIZES[:chunk]), SIZES[chunk] + (AUX if chunk == CHUNKS - 1 else 0))


def product(a, b):
    dims = (((1,), (1,)), ((), ()))

    def dot(u, v):
        return lax.dot_general(u, v, dims, preferred_element_type=jnp.float32)

    return dot(a[:, :D], b[:, :D]) + dot(a[:, :D], b[:, D:]) + dot(a[:, D:], b[:, :D])


def kernel(
    emb, lab_in, src_in, out,
    lab, src, raw, split, cols, row_acc, col_acc, part, part_in, stage, final,
    load_sem, lab_sem, src_sem, tree_send, tree_recv, sib_send, sib_recv, part_send, part_recv,
    row_send, row_recv, col_send, col_recv,
):
    row, col = lax.axis_index("row"), lax.axis_index("col")
    place = (col // 4, col % 4, row // 2)
    core = row % 2
    me = row * COLS_MESH + col

    def device(offset, flip=False):
        x, y, z = ((p + o) % 4 if o else p for p, o in zip(place, offset))
        c = (1 - core) if flip else core
        return (z * 2 + c, x * 4 + y)

    other_core = device((0, 0, 0), True)

    def remote(source, target, send, recv, to):
        return pltpu.make_async_remote_copy(
            src_ref=source, dst_ref=target, send_sem=send, recv_sem=recv,
            device_id=to, device_id_type=MESH,
        )

    load = pltpu.make_async_copy(emb, raw.at[0, pl.ds(0, ROWS)], load_sem)
    load.start()
    load_lab = pltpu.make_async_copy(lab_in, lab, lab_sem)
    load_lab.start()
    load_src = pltpu.make_async_copy(src_in, src, src_sem)
    load_src.start()
    barrier = pltpu.get_barrier_semaphore()
    for offset in DIRS:
        pl.semaphore_signal(barrier, inc=1, device_id=device(offset), device_id_type=MESH)
    pl.semaphore_signal(barrier, inc=1, device_id=other_core, device_id_type=MESH)

    load.wait()
    y = raw[0, pl.ds(0, ROWS)] * SCALE
    minus_half = -0.5 * jnp.sum(y * y, axis=1, keepdims=True)
    norm_row = jnp.transpose(jnp.broadcast_to(minus_half, (ROWS, 128)))[0:1]
    load_lab.wait()
    sign_row = (1 - 2 * lab[...]).astype(jnp.float32)
    aux = jnp.concatenate([norm_row, sign_row, jnp.zeros((AUX - 2, ROWS), jnp.float32)], axis=0)
    raw[0, pl.ds(ROWS, AUX)] = jnp.concatenate([aux, jnp.zeros((AUX, D - ROWS), jnp.float32)], axis=1)
    pl.semaphore_wait(barrier, 7)

    def relay(i, chunk):
        for w in CHILDREN[i]:
            sem = FIRST_SEM[w] + (chunk if CHILDREN[w] else 0)
            remote(
                raw.at[2 * i, span(chunk)], raw.at[2 * w, span(chunk)],
                tree_send, tree_recv.at[sem], device(minus(ORDER[i], ORDER[w])),
            ).start()

    def arrive(i, chunk):
        sem = FIRST_SEM[i] + (chunk if CHILDREN[i] else 0)
        rows = raw.at[2 * i, span(chunk)] if CHILDREN[i] else raw.at[2 * i]
        remote(rows, rows, tree_send, tree_recv.at[sem], other_core).wait_recv()

    def sibling(i):
        return remote(raw.at[2 * i], raw.at[2 * i + 1], sib_send, sib_recv.at[i], other_core)

    def prepare(slot):
        for start in range(0, ROWS, 32):
            rows = pl.ds(start, 32)
            y = raw[slot, rows] * SCALE
            high = y.astype(jnp.bfloat16)
            split[slot, rows, :D] = high
            split[slot, rows, D:] = (y - high.astype(jnp.float32)).astype(jnp.bfloat16)
        if slot % 2 == 0:
            aux = raw[slot, pl.ds(ROWS, AUX), :ROWS]
            cols[slot // 2] = jnp.transpose(jnp.concatenate([aux] * (128 // AUX), axis=0))

    def work(i, slots, both=True):
        a = split[2 * i]
        norm_i, sign_i = cols[i, :, 0:1], cols[i, :, 1:2]
        for slot in slots:
            g = product(a, split[slot])
            aux = raw[slot, pl.ds(ROWS, AUX), :ROWS]
            e = jnp.exp2(g + norm_i + aux[0:1])
            q = e * aux[1:2]
            row_acc[i] += q[:, :128] + q[:, 128:]
            if both:
                col_acc[slot] += jnp.sum((e * sign_i).reshape(ROWS // 8, 8, ROWS), axis=0)

    def half_slot(i, b):
        diff = minus(ORDER[i], ORDER[b])
        axis = [t for t in range(3) if diff[t] == 2][0]
        return 2 * b + place[axis] // 2

    def totals(i):
        for slot in (2 * i, 2 * i + 1):
            total = jnp.sum(col_acc[slot], axis=0, keepdims=True)
            if slot % 2 == 0:
                total = total + jnp.sum(jnp.transpose(row_acc[i]), axis=0, keepdims=True)
            part[slot] = total

    def send_totals(i):
        if i:
            rows = pl.ds(2 * i, 2)
            remote(
                part.at[rows], part_in.at[rows], part_send, part_recv, device(ORDER[i])
            ).start()

    for chunk in range(CHUNKS):
        relay(0, chunk)
    sibling(0).start()
    row_acc[...] = jnp.zeros_like(row_acc)
    col_acc[...] = jnp.zeros_like(col_acc)
    prepare(0)
    sibling(0).wait_recv()
    prepare(1)
    work(0, [0, 1], False)

    step, sent = 0, set()
    for op in PLAN:
        if op[0] == "fwd":
            arrive(op[1], op[2])
            relay(op[1], op[2])
            continue
        if op[0] == "share":
            if not CHILDREN[op[1]]:
                arrive(op[1], 0)
            if op[1] in SHARED:
                sibling(op[1]).start()
            continue
        _, i, full, half, own, other = op
        for w in other:
            sibling(w).wait_recv()
        done = [e for e in range(COUNT) if e not in sent and LAST[e] < step]
        for e in done:
            totals(e)
        for w in own:
            prepare(2 * w)
        for w in other:
            prepare(2 * w + 1)
        work(i, [2 * b + t for b in full for t in range(CORES)] + [half_slot(i, b) for b in half])
        for e in done:
            send_totals(e)
        sent.update(done)
        step += 1
    for e in range(COUNT):
        if e not in sent:
            totals(e)
            send_totals(e)

    rest = pl.ds(2, SLOTS - 2)
    arrived = remote(part.at[rest], part_in.at[rest], part_send, part_recv, other_core)
    arrived.wait_recv()
    mine, his = part[0], part[1]
    for i in range(1, COUNT):
        mine, his = mine + part_in[2 * i], his + part_in[2 * i + 1]
    mine, his = mine * (1000.0 / HALF_COUNT), his * (1000.0 / HALF_COUNT)
    his_sign = raw[1, pl.ds(ROWS, AUX), :ROWS][1:2]
    here = jnp.sum(mine * sign_row + his * his_sign, axis=1, keepdims=True)
    zero, one = jnp.where(core == 0, mine, his), jnp.where(core == 0, his, mine)
    tail = jnp.broadcast_to(here, (1, 128))
    stage[row] = jnp.concatenate(
        [jnp.concatenate([zero, tail], axis=1), jnp.concatenate([one, tail], axis=1)], axis=0
    )

    for k in range(1, ROWS_MESH):
        block = stage.at[row]
        remote(block, block, row_send, row_recv, ((row + k) % ROWS_MESH, col)).start()
    others = stage.at[pl.ds(1, ROWS_MESH - 1)]
    seven = remote(others, others, row_send, row_recv, other_core)
    seven.wait_recv()
    halves = [stage[2 * z] + stage[2 * z + 1] for z in range(ROWS_MESH // 2)]
    sums = jnp.concatenate(halves, axis=0)
    window = jnp.where(row < ROWS_MESH // 2, sums[:, :128], sums[:, 128:256])
    column_total = 0.5 * jnp.sum(sums[:, 256:], axis=0, keepdims=True)
    lane = lax.broadcasted_iota(jnp.int32, (8, 128), 1)
    base = (row % 4) * 32
    window = jnp.where((lane >= base) & (lane < base + 32), window, column_total)
    block = final.at[pl.ds(pl.multiple_of(col * 8, 8), 8)]
    final[pl.ds(pl.multiple_of(col * 8, 8), 8), :] = window
    for k in range(1, COLS_MESH):
        remote(block, block, col_send, col_recv, (row, (col + k) % COLS_MESH)).start()
    fifteen = remote(
        raw.at[0, pl.ds(0, 120), pl.ds(0, 128)], raw.at[0, pl.ds(0, 120), pl.ds(0, 128)],
        col_send, col_recv, other_core,
    )
    fifteen.wait_recv()

    values = final[...]
    lane = lax.broadcasted_iota(jnp.int32, values.shape, 1)
    first = jnp.sum(jnp.where(lane == base + 2 * col, values, 0.0), axis=1, keepdims=True)
    second = jnp.sum(jnp.where(lane == base + 2 * col + 1, values, 0.0), axis=1, keepdims=True)
    load_src.wait()
    ids = src[...]
    held = lax.broadcasted_iota(jnp.int32, (128, ROWS), 0)
    owner = (held % 8) * COLS_MESH + held // 8
    value = jnp.where((ids & 1) == 0, first, second)
    proofs = jnp.sum(jnp.where(owner == ids // ROWS, value, 0.0), axis=0, keepdims=True)
    unused = (base + 32) % 128
    sums = jnp.sum(jnp.where((lane == unused) & (held[:, :128] % 8 == 0), values, 0.0), axis=0, keepdims=True)
    total = jnp.sum(sums, axis=1, keepdims=True) * (1.0 / HALF_COUNT)
    out[...] = jnp.concatenate([proofs, jnp.broadcast_to(total, (1, 128))], axis=1)

    tree = raw.at[pl.ds(0, COUNT - 1)]
    remote(tree, tree, tree_send, load_sem, other_core).wait_send()
    shared = raw.at[pl.ds(0, len(SHARED))]
    remote(shared, shared, sib_send, load_sem, other_core).wait_send()
    arrived.wait_send()
    seven.wait_send()
    fifteen.wait_send()


def local(embeddings, labels, source_id):
    vmem = pl.BlockSpec(memory_space=pltpu.VMEM)
    dma = pltpu.SemaphoreType.DMA
    f32 = jnp.float32
    result = pl.pallas_call(
        kernel,
        out_shape=jax.ShapeDtypeStruct((1, ROWS + 128), f32),
        in_specs=[pl.BlockSpec(memory_space=pl.ANY)] * 3,
        out_specs=vmem,
        scratch_shapes=[
            pltpu.VMEM((1, ROWS), jnp.int32),
            pltpu.VMEM((1, ROWS), jnp.int32),
            pltpu.VMEM((SLOTS, ROWS + AUX, D), f32),
            pltpu.VMEM((SLOTS, ROWS, 2 * D), jnp.bfloat16),
            pltpu.VMEM((COUNT, ROWS, 128), f32),
            pltpu.VMEM((COUNT, ROWS, 128), f32),
            pltpu.VMEM((SLOTS, 8, ROWS), f32),
            pltpu.VMEM((SLOTS, 1, ROWS), f32),
            pltpu.VMEM((SLOTS, 1, ROWS), f32),
            pltpu.VMEM((ROWS_MESH, 2, ROWS + 128), f32),
            pltpu.VMEM((ROWS_MESH * COLS_MESH, 128), f32),
            dma, dma, dma, dma, dma((SEMS,)), dma, dma((COUNT,)), dma, dma, dma, dma, dma, dma,
        ],
        compiler_params=pltpu.CompilerParams(
            collective_id=0, has_side_effects=True, vmem_limit_bytes=56 * 2**20
        ),
    )(embeddings, labels.reshape(1, ROWS), source_id.reshape(1, ROWS))
    return result[0, :ROWS], result[0, ROWS]


def solution(mesh):
    return jax.shard_map(
        local,
        mesh=mesh,
        in_specs=(P(("row", "col"), None), P(("row", "col")), P(("row", "col"))),
        out_specs=(P(("row", "col")), P()),
        check_vma=False,
    )
```

```python
import math

import jax
import jax.numpy as jnp
from jax import lax
from jax.experimental import pallas as pl
from jax.experimental.pallas import tpu as pltpu
from jax.sharding import PartitionSpec as P

MESH = pl.DeviceIdType.MESH
D = 768
ROWS = 256
AUX = 8
CORES = 2
ROWS_MESH = 8
COLS_MESH = 16
HALF_COUNT = 16384
SCALE = math.sqrt(2.0 * math.log2(math.e) / 200.0)

SIZES = (40, 56, 56, 56, 48)
ORDER = [(0, 0, 0), (0, 0, 1), (0, 0, 3), (0, 3, 0), (3, 0, 0), (0, 1, 3), (1, 3, 0), (0, 0, 2), (0, 1, 2), (1, 2, 0), (2, 0, 0), (2, 2, 0)]
EDGES = [((0, 0, 0), (3, 0, 0)), ((0, 0, 0), (0, 0, 3)), ((0, 0, 0), (0, 3, 0)), ((0, 0, 0), (0, 0, 1)), ((0, 0, 3), (0, 1, 3)), ((0, 3, 0), (1, 3, 0)), ((3, 0, 0), (2, 0, 0)), ((0, 0, 1), (0, 0, 2)), ((0, 1, 3), (0, 1, 2)), ((1, 3, 0), (1, 2, 0)), ((1, 2, 0), (2, 2, 0))]
PLAN = [
    ('fwd', 1, 0),
    ('fwd', 2, 0),
    ('fwd', 3, 0),
    ('fwd', 4, 0),
    ('fwd', 1, 1),
    ('fwd', 2, 1),
    ('fwd', 3, 1),
    ('fwd', 4, 1),
    ('fwd', 5, 0),
    ('fwd', 6, 0),
    ('fwd', 1, 2),
    ('fwd', 2, 2),
    ('fwd', 3, 2),
    ('fwd', 4, 2),
    ('fwd', 5, 1),
    ('fwd', 6, 1),
    ('fwd', 1, 3),
    ('fwd', 2, 3),
    ('fwd', 3, 3),
    ('fwd', 4, 3),
    ('fwd', 5, 2),
    ('fwd', 6, 2),
    ('fwd', 1, 4),
    ('share', 1),
    ('fwd', 2, 4),
    ('share', 2),
    ('fwd', 3, 4),
    ('share', 3),
    ('fwd', 4, 4),
    ('share', 4),
    ('go', 1, (), (), (1,), ()),
    ('go', 1, (0,), (), (2,), ()),
    ('go', 3, (), (), (3,), (1,)),
    ('fwd', 9, 0),
    ('go', 2, (), (1,), (4,), (2,)),
    ('fwd', 5, 3),
    ('fwd', 6, 3),
    ('go', 3, (0, 1, 2), (), (), (3,)),
    ('go', 4, (0, 1, 2), (), (), (4,)),
    ('fwd', 5, 4),
    ('share', 5),
    ('fwd', 6, 4),
    ('share', 6),
    ('fwd', 9, 1),
    ('go', 4, (3,), (), (5,), ()),
    ('go', 5, (1, 3, 4), (), (6,), ()),
    ('fwd', 9, 2),
    ('go', 6, (1, 2, 4), (), (), (5,)),
    ('go', 6, (5,), (), (), (6,)),
    ('fwd', 9, 3),
    ('share', 7),
    ('share', 8),
    ('fwd', 9, 4),
    ('share', 9),
    ('share', 10),
    ('go', 7, (), (), (7,), ()),
    ('go', 7, (4, 6), (), (8,), ()),
    ('go', 8, (4, 6), (3,), (9,), (7,)),
    ('go', 9, (0, 1, 5), (4,), (10,), (8,)),
    ('go', 10, (1, 5, 6, 8), (0, 7), (), (10,)),
    ('share', 11),
    ('go', 11, (), (), (11,), ()),
    ('go', 11, (1, 5), (7, 10), (), ()),
]

DIRS = [(1, 0, 0), (3, 0, 0), (0, 1, 0), (0, 3, 0), (0, 0, 1), (0, 0, 3)]
COUNT = len(ORDER)
SLOTS = CORES * COUNT
INDEX = {e: i for i, e in enumerate(ORDER)}
CHUNKS = len(SIZES)
CHILDREN = {i: [INDEX[w] for u, w in EDGES if INDEX[u] == i] for i in range(COUNT)}
FIRST_SEM = {}
SEMS = 0
for _i in range(1, COUNT):
    FIRST_SEM[_i] = SEMS
    SEMS += CHUNKS if CHILDREN[_i] else 1
STEPS = [p for p in PLAN if p[0] == "go"]
SHARED = {0} | {b for p in STEPS for b in p[2] + p[3]}
LAST = {i: max([0] + [k for k, p in enumerate(STEPS) if (p[1] == i and p[2] + p[3]) or i in p[2] + p[3]]) for i in range(COUNT)}


def minus(a, b):
    return tuple((u - v) % 4 for u, v in zip(a, b))


def span(chunk):
    return pl.ds(sum(SIZES[:chunk]), SIZES[chunk] + (AUX if chunk == CHUNKS - 1 else 0))


def product(a, b):
    dims = (((1,), (1,)), ((), ()))

    def dot(u, v):
        return lax.dot_general(u, v, dims, preferred_element_type=jnp.float32)

    return dot(a[:, :D], b[:, :D]) + dot(a[:, :D], b[:, D:]) + dot(a[:, D:], b[:, :D])


def kernel(
    emb, lab_in, src_in, out,
    lab, src, raw, split, cols, row_acc, col_acc, part, part_in, stage, final,
    load_sem, lab_sem, src_sem, tree_send, tree_recv, sib_send, sib_recv, part_send, part_recv,
    row_send, row_recv, col_send, col_recv,
):
    row, col = lax.axis_index("row"), lax.axis_index("col")
    place = (col // 4, col % 4, row // 2)
    core = row % 2
    me = row * COLS_MESH + col

    def device(offset, flip=False):
        x, y, z = ((p + o) % 4 if o else p for p, o in zip(place, offset))
        c = (1 - core) if flip else core
        return (z * 2 + c, x * 4 + y)

    other_core = device((0, 0, 0), True)

    def remote(source, target, send, recv, to):
        return pltpu.make_async_remote_copy(
            src_ref=source, dst_ref=target, send_sem=send, recv_sem=recv,
            device_id=to, device_id_type=MESH,
        )

    load = pltpu.make_async_copy(emb, raw.at[0, pl.ds(0, ROWS)], load_sem)
    load.start()
    load_lab = pltpu.make_async_copy(lab_in, lab, lab_sem)
    load_lab.start()
    load_src = pltpu.make_async_copy(src_in, src, src_sem)
    load_src.start()
    barrier = pltpu.get_barrier_semaphore()
    for offset in DIRS:
        pl.semaphore_signal(barrier, inc=1, device_id=device(offset), device_id_type=MESH)
    pl.semaphore_signal(barrier, inc=1, device_id=other_core, device_id_type=MESH)

    load.wait()
    y = raw[0, pl.ds(0, ROWS)] * SCALE
    minus_half = -0.5 * jnp.sum(y * y, axis=1, keepdims=True)
    norm_row = jnp.transpose(jnp.broadcast_to(minus_half, (ROWS, 128)))[0:1]
    load_lab.wait()
    sign_row = (1 - 2 * lab[...]).astype(jnp.float32)
    aux = jnp.concatenate([norm_row, sign_row, jnp.zeros((AUX - 2, ROWS), jnp.float32)], axis=0)
    raw[0, pl.ds(ROWS, AUX)] = jnp.concatenate([aux, jnp.zeros((AUX, D - ROWS), jnp.float32)], axis=1)
    pl.semaphore_wait(barrier, 7)

    def relay(i, chunk):
        for w in CHILDREN[i]:
            sem = FIRST_SEM[w] + (chunk if CHILDREN[w] else 0)
            remote(
                raw.at[2 * i, span(chunk)], raw.at[2 * w, span(chunk)],
                tree_send, tree_recv.at[sem], device(minus(ORDER[i], ORDER[w])),
            ).start()

    def arrive(i, chunk):
        sem = FIRST_SEM[i] + (chunk if CHILDREN[i] else 0)
        rows = raw.at[2 * i, span(chunk)] if CHILDREN[i] else raw.at[2 * i]
        remote(rows, rows, tree_send, tree_recv.at[sem], other_core).wait_recv()

    def sibling(i):
        return remote(raw.at[2 * i], raw.at[2 * i + 1], sib_send, sib_recv.at[i], other_core)

    def prepare(slot):
        for start in range(0, ROWS, 32):
            rows = pl.ds(start, 32)
            y = raw[slot, rows] * SCALE
            high = y.astype(jnp.bfloat16)
            split[slot, rows, :D] = high
            split[slot, rows, D:] = (y - high.astype(jnp.float32)).astype(jnp.bfloat16)
        if slot % 2 == 0:
            aux = raw[slot, pl.ds(ROWS, AUX), :ROWS]
            cols[slot // 2] = jnp.transpose(jnp.concatenate([aux] * (128 // AUX), axis=0))

    def work(i, slots, both=True):
        a = split[2 * i]
        norm_i, sign_i = cols[i, :, 0:1], cols[i, :, 1:2]
        for slot in slots:
            g = product(a, split[slot])
            aux = raw[slot, pl.ds(ROWS, AUX), :ROWS]
            e = jnp.exp2(g + norm_i + aux[0:1])
            q = e * aux[1:2]
            row_acc[i] += q[:, :128] + q[:, 128:]
            if both:
                col_acc[slot] += jnp.sum((e * sign_i).reshape(ROWS // 8, 8, ROWS), axis=0)

    def half_slot(i, b):
        diff = minus(ORDER[i], ORDER[b])
        axis = [t for t in range(3) if diff[t] == 2][0]
        return 2 * b + place[axis] // 2

    def totals(i):
        for slot in (2 * i, 2 * i + 1):
            total = jnp.sum(col_acc[slot], axis=0, keepdims=True)
            if slot % 2 == 0:
                total = total + jnp.sum(jnp.transpose(row_acc[i]), axis=0, keepdims=True)
            part[slot] = total

    def send_totals(i):
        if i:
            rows = pl.ds(2 * i, 2)
            remote(
                part.at[rows], part_in.at[rows], part_send, part_recv, device(ORDER[i])
            ).start()

    for chunk in range(CHUNKS):
        relay(0, chunk)
    sibling(0).start()
    row_acc[...] = jnp.zeros_like(row_acc)
    col_acc[...] = jnp.zeros_like(col_acc)
    prepare(0)
    sibling(0).wait_recv()
    prepare(1)
    work(0, [0, 1], False)

    step, sent = 0, set()
    for op in PLAN:
        if op[0] == "fwd":
            arrive(op[1], op[2])
            relay(op[1], op[2])
            continue
        if op[0] == "share":
            if not CHILDREN[op[1]]:
                arrive(op[1], 0)
            if op[1] in SHARED:
                sibling(op[1]).start()
            continue
        _, i, full, half, own, other = op
        for w in other:
            sibling(w).wait_recv()
        done = [e for e in range(COUNT) if e not in sent and LAST[e] < step]
        for e in done:
            totals(e)
        for w in own:
            prepare(2 * w)
        for w in other:
            prepare(2 * w + 1)
        work(i, [2 * b + t for b in full for t in range(CORES)] + [half_slot(i, b) for b in half])
        for e in done:
            send_totals(e)
        sent.update(done)
        step += 1
    for e in range(COUNT):
        if e not in sent:
            totals(e)
            send_totals(e)

    rest = pl.ds(2, SLOTS - 2)
    arrived = remote(part.at[rest], part_in.at[rest], part_send, part_recv, other_core)
    arrived.wait_recv()
    mine, his = part[0], part[1]
    for i in range(1, COUNT):
        mine, his = mine + part_in[2 * i], his + part_in[2 * i + 1]
    mine, his = mine * (1000.0 / HALF_COUNT), his * (1000.0 / HALF_COUNT)
    his_sign = raw[1, pl.ds(ROWS, AUX), :ROWS][1:2]
    here = jnp.sum(mine * sign_row + his * his_sign, axis=1, keepdims=True)
    zero, one = jnp.where(core == 0, mine, his), jnp.where(core == 0, his, mine)
    tail = jnp.broadcast_to(here, (1, 128))
    stage[row] = jnp.concatenate(
        [jnp.concatenate([zero, tail], axis=1), jnp.concatenate([one, tail], axis=1)], axis=0
    )

    for k in range(1, ROWS_MESH):
        block = stage.at[row]
        remote(block, block, row_send, row_recv, ((row + k) % ROWS_MESH, col)).start()
    others = stage.at[pl.ds(1, ROWS_MESH - 1)]
    seven = remote(others, others, row_send, row_recv, other_core)
    seven.wait_recv()
    halves = [stage[2 * z] + stage[2 * z + 1] for z in range(ROWS_MESH // 2)]
    sums = jnp.concatenate(halves, axis=0)
    window = jnp.where(row < ROWS_MESH // 2, sums[:, :128], sums[:, 128:256])
    column_total = 0.5 * jnp.sum(sums[:, 256:], axis=0, keepdims=True)
    lane = lax.broadcasted_iota(jnp.int32, (8, 128), 1)
    base = (row % 4) * 32
    window = jnp.where((lane >= base) & (lane < base + 32), window, column_total)
    block = final.at[pl.ds(pl.multiple_of(col * 8, 8), 8)]
    final[pl.ds(pl.multiple_of(col * 8, 8), 8), :] = window
    for k in range(1, COLS_MESH):
        remote(block, block, col_send, col_recv, (row, (col + k) % COLS_MESH)).start()
    fifteen = remote(
        raw.at[0, pl.ds(0, 120), pl.ds(0, 128)], raw.at[0, pl.ds(0, 120), pl.ds(0, 128)],
        col_send, col_recv, other_core,
    )
    fifteen.wait_recv()

    values = final[...]
    lane = lax.broadcasted_iota(jnp.int32, values.shape, 1)
    first = jnp.sum(jnp.where(lane == base + 2 * col, values, 0.0), axis=1, keepdims=True)
    second = jnp.sum(jnp.where(lane == base + 2 * col + 1, values, 0.0), axis=1, keepdims=True)
    load_src.wait()
    ids = src[...]
    held = lax.broadcasted_iota(jnp.int32, (128, ROWS), 0)
    owner = (held % 8) * COLS_MESH + held // 8
    value = jnp.where((ids & 1) == 0, first, second)
    proofs = jnp.sum(jnp.where(owner == ids // ROWS, value, 0.0), axis=0, keepdims=True)
    unused = (base + 32) % 128
    sums = jnp.sum(jnp.where((lane == unused) & (held[:, :128] % 8 == 0), values, 0.0), axis=0, keepdims=True)
    total = jnp.sum(sums, axis=1, keepdims=True) * (1.0 / HALF_COUNT)
    out[...] = jnp.concatenate([proofs, jnp.broadcast_to(total, (1, 128))], axis=1)

    tree = raw.at[pl.ds(0, COUNT - 1)]
    remote(tree, tree, tree_send, load_sem, other_core).wait_send()
    shared = raw.at[pl.ds(0, len(SHARED))]
    remote(shared, shared, sib_send, load_sem, other_core).wait_send()
    arrived.wait_send()
    seven.wait_send()
    fifteen.wait_send()


def local(embeddings, labels, source_id):
    vmem = pl.BlockSpec(memory_space=pltpu.VMEM)
    dma = pltpu.SemaphoreType.DMA
    f32 = jnp.float32
    result = pl.pallas_call(
        kernel,
        out_shape=jax.ShapeDtypeStruct((1, ROWS + 128), f32),
        in_specs=[pl.BlockSpec(memory_space=pl.ANY)] * 3,
        out_specs=vmem,
        scratch_shapes=[
            pltpu.VMEM((1, ROWS), jnp.int32),
            pltpu.VMEM((1, ROWS), jnp.int32),
            pltpu.VMEM((SLOTS, ROWS + AUX, D), f32),
            pltpu.VMEM((SLOTS, ROWS, 2 * D), jnp.bfloat16),
            pltpu.VMEM((COUNT, ROWS, 128), f32),
            pltpu.VMEM((COUNT, ROWS, 128), f32),
            pltpu.VMEM((SLOTS, 8, ROWS), f32),
            pltpu.VMEM((SLOTS, 1, ROWS), f32),
            pltpu.VMEM((SLOTS, 1, ROWS), f32),
            pltpu.VMEM((ROWS_MESH, 2, ROWS + 128), f32),
            pltpu.VMEM((ROWS_MESH * COLS_MESH, 128), f32),
            dma, dma, dma, dma, dma((SEMS,)), dma, dma((COUNT,)), dma, dma, dma, dma, dma, dma,
        ],
        compiler_params=pltpu.CompilerParams(
            collective_id=0, has_side_effects=True, vmem_limit_bytes=56 * 2**20
        ),
    )(embeddings, labels.reshape(1, ROWS), source_id.reshape(1, ROWS))
    return result[0, :ROWS], result[0, ROWS]


def solution(mesh):
    return jax.shard_map(
        local,
        mesh=mesh,
        in_specs=(P(("row", "col"), None), P(("row", "col")), P(("row", "col"))),
        out_specs=(P(("row", "col")), P()),
        check_vma=False,
    )
```
